32 devices in a mesh: blk: 8 (over y, x, core), pw: 4 (over z).
Axes of the slice: x: 2, y: 2, z: 4, core: 2. Of those that a mesh axis runs over, the one named last changes fastest.
Arguments:
- res_pair: bfloat16 [16384, 12288], P('blk', 'pw'), may hold values from -0.56640625 to 0.56640625
- band_pair: bfloat16 [2048, 12288], P('blk', 'pw'), may hold values from -0.56640625 to 0.56640625
- coulomb: float32 [12288], P('pw'), may hold values from 0.2 to 5
- screening: float32 [2048], P('pw'), may hold values from 0.2 to 5
- val_form: bfloat16 [400, 2048], P(None, 'pw'), may hold values from -2.3125 to 2.3125
- cond_form: bfloat16 [600, 2048], P(None, 'pw'), may hold values from -2.3125 to 2.3125
- res_bands: int32 [3, 16384], P(None, 'blk'), may hold values from 0 to 299, as said below
- band_bands: int32 [3, 2048], P(None, 'blk'), may hold values from 0 to 299, as said below
Outputs:
- kernel: float32 [2, 16384, 256], P(None, ('blk', 'pw'))
The draws below stay inside these ranges and needn't reach their ends.
Inputs may be any that keep to these rules, and one draw needn't show every extreme that they name: `res_bands`: row 0 holds valence bands below 200, row 1 conduction bands below 300, row 2 k-points below 2. `band_bands`: row 0 holds valence bands below 200, row 1 conduction bands below 300, row 2 k-points below 2.
All inputs are finite; a program needn't handle non-finite values.
Results may differ from the reference program's by a relative error of at most 0.01.
Values may be sent and summed in bfloat16 or wider, within the bound.
A program may use at most 64 MiB of HBM per device.

```python
import math
import jax
import jax.numpy as jnp
from jax import lax

NPW = 12288
NGW = 2048
NV = 200
NC = 300
NK = 2
RES = 2048
VB = 256
STEPS = 2
TRANS = 16384
BAND = 2048
N_BLK = 8
N_PW = 4


def draw_bands(key, count):
    first, second, third = jax.random.split(key, 3)
    valence = jax.random.randint(first, (count,), 0, NV, dtype=jnp.int32)
    conduct = jax.random.randint(second, (count,), 0, NC, dtype=jnp.int32)
    kpoint = jax.random.randint(third, (count,), 0, NK, dtype=jnp.int32)
    return jnp.stack([valence, conduct, kpoint], axis=0)


def draw_res_bands(key, part):
    key = jax.random.fold_in(key, 11)
    return draw_bands(key, TRANS)


def draw_band_bands(key, part):
    key = jax.random.fold_in(key, 23)
    return draw_bands(key, BAND)


def steps_of(rng, dims, cuts, least, largest):
    loudness = 1.0
    for dim, blocks in cuts:
        draws = jax.random.uniform(jax.random.fold_in(jax.random.fold_in(rng, 6), dim), (blocks,), jnp.float32, least / len(cuts), largest / len(cuts))
        loudness = loudness * jnp.repeat(jnp.exp(draws), dims[dim] // blocks).reshape((-1,) + (1,) * (len(dims) - 1 - dim))
    return loudness


def bell_draw(key, extent, deviation, most, cuts=(), kind=jnp.bfloat16):
    level = steps_of(key, extent, cuts, -0.22, 0.18) if cuts else 1.0
    drawn = jax.random.normal(key, extent, jnp.float32) * deviation * level
    return jnp.minimum(jnp.maximum(drawn, -most), most).astype(kind)


def setup_inputs(seed: int = 0) -> dict:
    key_of = jax.random.split(jax.random.key(seed), 9)
    return {
        "res_pair": bell_draw(key_of[0], (TRANS, NPW), (NPW ** -0.25), 0.56640625, ((0, 8), (1, 4))),
        "band_pair": bell_draw(key_of[1], (BAND, NPW), (NPW ** -0.25), 0.56640625, ((0, 8), (1, 4))),
        "coulomb": jnp.clip(jnp.exp(math.log(5.0) - 3.218876 * jax.random.uniform(key_of[2], (NPW,), jnp.float32) ** steps_of(key_of[2], (NPW,), ((0, 4),), -0.2, 0.2)), 0.2, 5.0),
        "screening": jnp.clip(jnp.exp(math.log(5.0) - 3.218876 * jax.random.uniform(key_of[3], (NGW,), jnp.float32) ** steps_of(key_of[3], (NGW,), ((0, 4),), -0.2, 0.2)), 0.2, 5.0),
        "val_form": bell_draw(key_of[4], (NK * NV, NGW), (NGW ** -0.125), 2.3125, ((1, 4),)),
        "cond_form": bell_draw(key_of[5], (NK * NC, NGW), (NGW ** -0.125), 2.3125, ((1, 4),)),
        "res_bands": draw_res_bands(jax.random.fold_in(key_of[8], 71), 0),
        "band_bands": draw_band_bands(jax.random.fold_in(key_of[8], 71), 0),
    }


def make_density(bands, val_form, cond_form):
    rows_val = bands[2] * NV + bands[0]
    rows_cond = bands[2] * NC + bands[1]
    valence = jnp.take(val_form, rows_val.astype(jnp.int32), axis=0).astype(jnp.float32)
    conduct = jnp.take(cond_form, rows_cond.astype(jnp.int32), axis=0).astype(jnp.float32)
    return (valence * conduct).astype(jnp.bfloat16)


def reference(res_pair, band_pair, coulomb, screening, val_form, cond_form, res_bands, band_bands):
    highest = lax.Precision.HIGHEST
    res_density = make_density(res_bands, val_form, cond_form)
    band_density = make_density(band_bands, val_form, cond_form)
    weighted = (band_pair.astype(jnp.float32) * coulomb[None, :]).astype(jnp.bfloat16)
    screened = (band_density.astype(jnp.float32) * screening[None, :]).astype(jnp.bfloat16)
    pair_groups = NPW // N_PW
    screen_groups = NGW // N_PW

    def one_block(block_index):
        start = (block_index * RES).astype(jnp.int32)
        pair_rows = lax.dynamic_slice_in_dim(res_pair, start, RES, 0).astype(jnp.float32)
        dens_rows = lax.dynamic_slice_in_dim(res_density, start, RES, 0).astype(jnp.float32)
        pair_rows = pair_rows.reshape(RES, N_PW, pair_groups)
        dens_rows = dens_rows.reshape(RES, N_PW, screen_groups)
        results = []
        for step_index in range(1, STEPS + 1):
            other = ((block_index - step_index) % N_BLK) * VB
            other = other.astype(jnp.int32)
            vis_weight = lax.dynamic_slice_in_dim(weighted, other, VB, 0).astype(jnp.float32)
            vis_screen = lax.dynamic_slice_in_dim(screened, other, VB, 0).astype(jnp.float32)
            vis_weight = vis_weight.reshape(VB, N_PW, pair_groups)
            vis_screen = vis_screen.reshape(VB, N_PW, screen_groups)
            exchange_part = jnp.einsum("rpg,bpg->prb", pair_rows, vis_weight, precision=highest)
            direct_part = jnp.einsum("rpg,bpg->prb", dens_rows, vis_screen, precision=highest)
            partial_terms = 2.0 * exchange_part - direct_part
            results.append(jnp.sum(partial_terms, axis=0))
        return jnp.stack(results, axis=0)

    blocks = lax.map(one_block, jnp.arange(N_BLK, dtype=jnp.int32))
    return jnp.transpose(blocks, (1, 0, 2, 3)).reshape(STEPS, N_BLK * RES, VB)
```

```python
import functools

import jax
import jax.numpy as jnp
from jax import lax
from jax.experimental import pallas as pl
from jax.experimental.pallas import tpu as pltpu
from jax.sharding import PartitionSpec as P

NV = 200
NC = 300
STEPS = 2
LANES = 128
GROUP = 256
MESH = pl.DeviceIdType.MESH


def rounded_up(count, unit):
    return (count + unit - 1) // unit * unit


def kernel(
    n_blk, n_pw, n_val,
    res_hbm, band_ref, coul_ref, scr_ref, forms_ref, res_bands, band_bands, out_ref,
    res, res_sem, dens, bidx, idx_in, wgt, rhs, rhs_scr, part, up_in, dn_in, up_out, dn_out, final,
    idx_send, idx_recv, near_send, far_send, fwd_send, rhs_recv,
    up_send, up_recv, dn_send, dn_recv,
):
    chunks, rows = wgt.shape[0], wgt.shape[1]
    own_rows = out_ref.shape[1]
    me = lax.axis_index("blk")
    w = lax.axis_index("pw")
    even = lax.rem(me, 2) == 0
    one_on, two_on = lax.rem(me + 1, n_blk), lax.rem(me + 2, n_blk)
    one_back, two_back = lax.rem(me + n_blk - 1, n_blk), lax.rem(me + n_blk - 2, n_blk)

    load = pltpu.make_async_copy(res_hbm, res, res_sem)
    load.start()

    barrier = pltpu.get_barrier_semaphore()
    for other in (one_on, two_on, one_back, two_back):
        pl.semaphore_signal(barrier, inc=1, device_id=(other, w), device_id_type=MESH)

    @pl.when(w > 0)
    def _():
        pl.semaphore_signal(barrier, inc=1, device_id=(me, w - 1), device_id_type=MESH)

    @pl.when(w < n_pw - 1)
    def _():
        pl.semaphore_signal(barrier, inc=1, device_id=(me, w + 1), device_id_type=MESH)

    peers = 4 + jnp.where(w > 0, 1, 0) + jnp.where(w < n_pw - 1, 1, 0)
    pl.semaphore_wait(barrier, peers)

    def remote(src, dst, send, recv, blk, pw):
        return pltpu.make_async_remote_copy(
            src_ref=src, dst_ref=dst, send_sem=send, recv_sem=recv,
            device_id=(blk, pw), device_id_type=MESH,
        )

    def send_index(slot, target):
        return remote(bidx, idx_in.at[slot], idx_send.at[slot], idx_recv.at[slot], target, w)

    def send_near(c):
        return remote(wgt.at[c], rhs.at[c, 0], near_send.at[c], rhs_recv.at[c, 0], one_on, w)

    def send_far(c):
        return remote(wgt.at[c], rhs.at[c, 1], far_send.at[c], rhs_recv.at[c, 1], two_on, w)

    def forward(c):
        return remote(rhs.at[c, 0], rhs.at[c, 1], fwd_send.at[c], rhs_recv.at[c, 1], one_on, w)

    def send_up(c, q):
        return remote(up_out.at[c, q], up_in.at[c, q], up_send.at[c, q], up_recv.at[c, q], me, w + 1)

    def send_dn(c, q):
        return remote(dn_out.at[c, q], dn_in.at[c, q], dn_send.at[c, q], dn_recv.at[c, q], me, w - 1)

    bidx[...] = jnp.zeros_like(bidx)
    bidx[0:1, :] = band_bands[2:3, :] * NV + band_bands[0:1, :]
    bidx[1:2, :] = band_bands[2:3, :] * NC + band_bands[1:2, :]
    send_index(0, one_on).start()
    send_index(1, two_on).start()

    @pl.loop(0, chunks)
    def _(c):
        block = band_ref[pl.ds(pl.multiple_of(c * rows, rows), rows), :].astype(jnp.float32)
        wgt[c] = (block * (2.0 * coul_ref[...])).astype(jnp.bfloat16)
        send_near(c).start()

        @pl.when(even)
        def _():
            send_far(c).start()

    val_depth = rounded_up(n_val, LANES)
    cond_from = n_val // LANES * LANES
    cond_depth = forms_ref.shape[0] - cond_from

    def one_hot(row, depth):
        column = jnp.concatenate(
            [
                jnp.broadcast_to(row[:, h * LANES:(h + 1) * LANES], (LANES, LANES)).T
                for h in range(GROUP // LANES)
            ],
            axis=0,
        )
        lane = lax.broadcasted_iota(jnp.int32, (GROUP, LANES), 1)
        return jnp.concatenate(
            [
                jnp.where(column == lane + start, 1.0, 0.0).astype(jnp.bfloat16)
                for start in range(0, depth, LANES)
            ],
            axis=1,
        )

    def density(val_row, cond_row):
        valence = jnp.dot(
            one_hot(val_row, val_depth), forms_ref[:val_depth, :], preferred_element_type=jnp.float32
        )
        conduct = jnp.dot(
            one_hot(cond_row + (n_val - cond_from), cond_depth), forms_ref[cond_from:, :],
            preferred_element_type=jnp.float32,
        )
        return (valence * conduct).astype(jnp.bfloat16)

    @pl.loop(0, dens.shape[0] // GROUP)
    def _(g):
        at = pl.ds(pl.multiple_of(g * GROUP, GROUP), GROUP)
        point = res_bands[2:3, at]
        dens[at, :] = density(point * NV + res_bands[0:1, at], point * NC + res_bands[1:2, at])

    for slot, target in ((0, one_on), (1, two_on)):
        send_index(slot, target).wait_recv()
        for g in range(chunks * rows // GROUP):
            at = slice(g * GROUP, (g + 1) * GROUP)
            block = density(idx_in[slot, 0:1, at], idx_in[slot, 1:2, at])
            block = (block.astype(jnp.float32) * (-scr_ref[...])).astype(jnp.bfloat16)
            for h in range(GROUP // rows):
                rhs_scr[g * (GROUP // rows) + h, slot] = block[h * rows:(h + 1) * rows, :]

    load.wait()

    def multiply(c):
        send_near(c).wait_recv()

        @pl.when(even)
        def _():
            forward(c).start()

        send_far(c).wait_recv()
        weighted = rhs[c].reshape(2 * rows, rhs.shape[3])
        screened = rhs_scr[c].reshape(2 * rows, rhs_scr.shape[3])

        @pl.loop(0, n_pw)
        def _(j):
            q = jnp.where(2 * w < n_pw, n_pw - 1 - j, j)
            at = pl.ds(pl.multiple_of(q * own_rows, own_rows), own_rows)
            contract = (((1,), (1,)), ((), ()))
            term = lax.dot_general(
                res[at, :], weighted, contract, preferred_element_type=jnp.float32
            ) + lax.dot_general(
                dens[at, :], screened, contract, preferred_element_type=jnp.float32
            )
            part[lax.rem(c, 2), q] = term

            @pl.when(jnp.logical_and(w == 0, q > 0))
            def _():
                up_out[c, q] = term.astype(jnp.bfloat16)
                send_up(c, q).start()

            @pl.when(jnp.logical_and(w == n_pw - 1, q < n_pw - 1))
            def _():
                dn_out[c, q] = term.astype(jnp.bfloat16)
                send_dn(c, q).start()

    def relay(c):
        slot = lax.rem(c, 2)

        def upward():
            @pl.when(w > 0)
            def _():
                @pl.loop(0, n_pw - 1 - w)
                def _(j):
                    q = n_pw - 1 - j
                    send_up(c, q).wait_recv()
                    total = part[slot, q] + up_in[c, q].astype(jnp.float32)
                    up_out[c, q] = total.astype(jnp.bfloat16)
                    send_up(c, q).start()

        def downward():
            @pl.when(w < n_pw - 1)
            def _():
                @pl.loop(0, w)
                def _(q):
                    send_dn(c, q).wait_recv()
                    total = part[slot, q] + dn_in[c, q].astype(jnp.float32)
                    dn_out[c, q] = total.astype(jnp.bfloat16)
                    send_dn(c, q).start()

        @pl.when(2 * w < n_pw)
        def _():
            upward()
            downward()

        @pl.when(2 * w >= n_pw)
        def _():
            downward()
            upward()

        final[c] = part[slot, w]

        @pl.when(w > 0)
        def _():
            send_up(c, w).wait_recv()
            final[c] += up_in[c, w].astype(jnp.float32)

        @pl.when(w < n_pw - 1)
        def _():
            send_dn(c, w).wait_recv()
            final[c] += dn_in[c, w].astype(jnp.float32)

    @pl.loop(0, chunks)
    def _(c):
        multiply(c)

        @pl.when(c > 0)
        def _():
            relay(c - 1)

    relay(chunks - 1)

    for c in range(chunks):
        for s in range(STEPS):
            out_ref[s, :, c * rows:(c + 1) * rows] = final[c][:, s * rows:(s + 1) * rows]

    send_index(0, one_on).wait_send()
    send_index(1, two_on).wait_send()

    @pl.loop(0, chunks)
    def _(c):
        send_near(c).wait_send()

        @pl.when(even)
        def _():
            send_far(c).wait_send()
            forward(c).wait_send()

        @pl.when(w < n_pw - 1)
        def _():
            @pl.loop(w + 1, n_pw)
            def _(q):
                send_up(c, q).wait_send()

        @pl.when(w > 0)
        def _():
            @pl.loop(0, w)
            def _(q):
                send_dn(c, q).wait_send()


def local(n_blk, n_pw, res_pair, band_pair, coulomb, screening, val_form, cond_form, res_bands, band_bands):
    n_res, depth = res_pair.shape
    n_band = band_pair.shape[0]
    width = val_form.shape[1]
    n_val, n_cond = val_form.shape[0], cond_form.shape[0]
    chunks = 4 if n_pw <= 4 else 2
    rows = n_band // chunks
    own_rows = n_res // n_pw
    spare = rounded_up(n_val + n_cond, LANES) - n_val - n_cond
    forms = jnp.concatenate([val_form, cond_form, jnp.zeros((spare, width), val_form.dtype)], axis=0)
    bf16, f32, i32 = jnp.bfloat16, jnp.float32, jnp.int32
    dma = pltpu.SemaphoreType.DMA
    vmem = pl.BlockSpec(memory_space=pltpu.VMEM)
    return pl.pallas_call(
        functools.partial(kernel, n_blk, n_pw, n_val),
        out_shape=jax.ShapeDtypeStruct((STEPS, own_rows, n_band), f32),
        in_specs=[pl.BlockSpec(memory_space=pl.ANY)] + [vmem] * 6,
        out_specs=vmem,
        scratch_shapes=[
            pltpu.VMEM((n_res, depth), bf16),
            dma(()),
            pltpu.VMEM((n_res, width), bf16),
            pltpu.VMEM((8, n_band), i32),
            pltpu.VMEM((2, 8, n_band), i32),
            pltpu.VMEM((chunks, rows, depth), bf16),
            pltpu.VMEM((chunks, 2, rows, depth), bf16),
            pltpu.VMEM((chunks, 2, rows, width), bf16),
            pltpu.VMEM((2, n_pw, own_rows, 2 * rows), f32),
            pltpu.VMEM((chunks, n_pw, own_rows, 2 * rows), bf16),
            pltpu.VMEM((chunks, n_pw, own_rows, 2 * rows), bf16),
            pltpu.VMEM((chunks, n_pw, own_rows, 2 * rows), bf16),
            pltpu.VMEM((chunks, n_pw, own_rows, 2 * rows), bf16),
            pltpu.VMEM((chunks, own_rows, 2 * rows), f32),
            dma((2,)),
            dma((2,)),
            dma((chunks,)),
            dma((chunks,)),
            dma((chunks,)),
            dma((chunks, 2)),
            dma((chunks, n_pw)),
            dma((chunks, n_pw)),
            dma((chunks, n_pw)),
            dma((chunks, n_pw)),
        ],
        compiler_params=pltpu.CompilerParams(
            collective_id=0, has_side_effects=True, vmem_limit_bytes=56 * 1024 * 1024
        ),
        cost_estimate=pl.CostEstimate(
            flops=2 * STEPS * n_res * n_band * (depth + width),
            bytes_accessed=2 * n_res * depth,
            transcendentals=0,
        ),
        name="kernel_blocks",
    )(res_pair, band_pair, coulomb[None, :], screening[None, :], forms, res_bands, band_bands)


def solution(mesh):
    return jax.shard_map(
        functools.partial(local, mesh.shape["blk"], mesh.shape["pw"]),
        mesh=mesh,
        in_specs=(
            P("blk", "pw"),
            P("blk", "pw"),
            P("pw"),
            P("pw"),
            P(None, "pw"),
            P(None, "pw"),
            P(None, "blk"),
            P(None, "blk"),
        ),
        out_specs=P(None, ("blk", "pw"), None),
        check_vma=False,
    )
```

```python
import functools

import jax
import jax.numpy as jnp
from jax import lax
from jax.experimental import pallas as pl
from jax.experimental.pallas import tpu as pltpu
from jax.sharding import PartitionSpec as P

NV = 200
NC = 300
STEPS = 2
LANES = 128
GROUP = 256
MESH = pl.DeviceIdType.MESH


def rounded_up(count, unit):
    return (count + unit - 1) // unit * unit


def kernel(
    n_blk, n_pw,
    res_hbm, band_ref, coul_ref, scr_ref, val_form, cond_form, res_bands, band_bands, out_ref,
    res, res_sem, val_pad, cond_pad, dens, bidx, idx_in, wgt, rhs, rhs_scr, part, up_in, dn_in, up_out, dn_out, final,
    idx_send, idx_recv, near_send, far_send, fwd_send, rhs_recv,
    up_send, up_recv, dn_send, dn_recv,
):
    chunks, rows = wgt.shape[0], wgt.shape[1]
    own_rows = out_ref.shape[1]
    me = lax.axis_index("blk")
    w = lax.axis_index("pw")
    even = lax.rem(me, 2) == 0
    one_on, two_on = lax.rem(me + 1, n_blk), lax.rem(me + 2, n_blk)
    one_back, two_back = lax.rem(me + n_blk - 1, n_blk), lax.rem(me + n_blk - 2, n_blk)

    load = pltpu.make_async_copy(res_hbm, res, res_sem)
    load.start()

    barrier = pltpu.get_barrier_semaphore()
    for other in (one_on, two_on, one_back, two_back):
        pl.semaphore_signal(barrier, inc=1, device_id=(other, w), device_id_type=MESH)

    @pl.when(w > 0)
    def _():
        pl.semaphore_signal(barrier, inc=1, device_id=(me, w - 1), device_id_type=MESH)

    @pl.when(w < n_pw - 1)
    def _():
        pl.semaphore_signal(barrier, inc=1, device_id=(me, w + 1), device_id_type=MESH)

    peers = 4 + jnp.where(w > 0, 1, 0) + jnp.where(w < n_pw - 1, 1, 0)
    pl.semaphore_wait(barrier, peers)

    def remote(src, dst, send, recv, blk, pw):
        return pltpu.make_async_remote_copy(
            src_ref=src, dst_ref=dst, send_sem=send, recv_sem=recv,
            device_id=(blk, pw), device_id_type=MESH,
        )

    def send_index(slot, target):
        return remote(bidx, idx_in.at[slot], idx_send.at[slot], idx_recv.at[slot], target, w)

    def send_near(c):
        return remote(wgt.at[c], rhs.at[0, c], near_send.at[c], rhs_recv.at[0, c], one_on, w)

    def send_far(c):
        return remote(wgt.at[c], rhs.at[1, c], far_send.at[c], rhs_recv.at[1, c], two_on, w)

    def forward(c):
        return remote(rhs.at[0, c], rhs.at[1, c], fwd_send.at[c], rhs_recv.at[1, c], one_on, w)

    def send_up(c, q):
        return remote(up_out.at[c, q], up_in.at[c, q], up_send.at[c, q], up_recv.at[c, q], me, w + 1)

    def send_dn(c, q):
        return remote(dn_out.at[c, q], dn_in.at[c, q], dn_send.at[c, q], dn_recv.at[c, q], me, w - 1)

    bidx[...] = jnp.zeros_like(bidx)
    bidx[0:1, :] = band_bands[2:3, :] * NV + band_bands[0:1, :]
    bidx[1:2, :] = band_bands[2:3, :] * NC + band_bands[1:2, :]
    send_index(0, one_on).start()
    send_index(1, two_on).start()

    @pl.loop(0, chunks)
    def _(c):
        block = band_ref[pl.ds(pl.multiple_of(c * rows, rows), rows), :].astype(jnp.float32)
        wgt[c] = (block * (2.0 * coul_ref[...])).astype(jnp.bfloat16)
        send_near(c).start()

        @pl.when(even)
        def _():
            send_far(c).start()

    for form, padded in ((val_form, val_pad), (cond_form, cond_pad)):
        spare = jnp.zeros((padded.shape[0] - form.shape[0], form.shape[1]), jnp.float32)
        padded[...] = jnp.concatenate([form[...].astype(jnp.float32), spare], axis=0).astype(padded.dtype)

    def one_hot(row, depth):
        column = jnp.concatenate(
            [
                jnp.broadcast_to(row[:, h * LANES:(h + 1) * LANES], (LANES, LANES)).T
                for h in range(GROUP // LANES)
            ],
            axis=0,
        )
        lane = lax.broadcasted_iota(jnp.int32, (GROUP, LANES), 1)
        return jnp.concatenate(
            [
                jnp.where(column == lane + start, 1.0, 0.0).astype(jnp.bfloat16)
                for start in range(0, depth, LANES)
            ],
            axis=1,
        )

    def density(val_row, cond_row):
        valence = jnp.dot(
            one_hot(val_row, val_pad.shape[0]), val_pad[...], preferred_element_type=jnp.float32
        )
        conduct = jnp.dot(
            one_hot(cond_row, cond_pad.shape[0]), cond_pad[...], preferred_element_type=jnp.float32
        )
        return (valence * conduct).astype(jnp.bfloat16)

    @pl.loop(0, dens.shape[0] // GROUP)
    def _(g):
        at = pl.ds(pl.multiple_of(g * GROUP, GROUP), GROUP)
        point = res_bands[2:3, at]
        dens[at, :] = density(point * NV + res_bands[0:1, at], point * NC + res_bands[1:2, at])

    for slot, target in ((0, one_on), (1, two_on)):
        send_index(slot, target).wait_recv()
        for g in range(chunks * rows // GROUP):
            at = slice(g * GROUP, (g + 1) * GROUP)
            block = density(idx_in[slot, 0:1, at], idx_in[slot, 1:2, at])
            block = (block.astype(jnp.float32) * (-scr_ref[...])).astype(jnp.bfloat16)
            for h in range(GROUP // rows):
                rhs_scr[slot, g * (GROUP // rows) + h] = block[h * rows:(h + 1) * rows, :]

    load.wait()

    half = chunks // 2

    def parts_of(c):
        slot, unit = c // half, 2 * (c % half)
        return (
            (jnp.where(even, 0, slot), jnp.where(even, c, unit)),
            (jnp.where(even, 1, slot), jnp.where(even, c, unit + 1)),
        )

    def landed(slot, unit):
        remote(wgt.at[0], rhs.at[slot, unit], near_send.at[0], rhs_recv.at[slot, unit], one_on, w).wait_recv()

    def packed(term):
        if 2 * rows >= LANES:
            return term
        fold = LANES // (2 * rows)
        tall = own_rows // fold
        return jnp.concatenate([term[f * tall:(f + 1) * tall] for f in range(fold)], axis=1)

    def multiply(c):
        first, second = parts_of(c)
        landed(*first)

        @pl.when(even)
        def _():
            forward(c).start()

        landed(*second)
        weighted = jnp.concatenate([rhs[first], rhs[second]], axis=0)
        screened = jnp.concatenate([rhs_scr[first], rhs_scr[second]], axis=0)

        @pl.loop(0, n_pw)
        def _(j):
            q = jnp.where(2 * w < n_pw, n_pw - 1 - j, j)
            at = pl.ds(pl.multiple_of(q * own_rows, own_rows), own_rows)
            contract = (((1,), (1,)), ((), ()))
            term = lax.dot_general(
                res[at, :], weighted, contract, preferred_element_type=jnp.float32
            ) + lax.dot_general(
                dens[at, :], screened, contract, preferred_element_type=jnp.float32
            )
            term = packed(term)
            part[lax.rem(c, 2), q] = term

            @pl.when(jnp.logical_and(w == 0, q > 0))
            def _():
                up_out[c, q] = term.astype(jnp.bfloat16)
                send_up(c, q).start()

            @pl.when(jnp.logical_and(w == n_pw - 1, q < n_pw - 1))
            def _():
                dn_out[c, q] = term.astype(jnp.bfloat16)
                send_dn(c, q).start()

    def upward(c):
        @pl.when(w > 0)
        def _():
            @pl.loop(0, n_pw - 1 - w)
            def _(j):
                q = n_pw - 1 - j
                send_up(c, q).wait_recv()
                total = part[lax.rem(c, 2), q] + up_in[c, q].astype(jnp.float32)
                up_out[c, q] = total.astype(jnp.bfloat16)
                send_up(c, q).start()

    def downward(c):
        @pl.when(w < n_pw - 1)
        def _():
            @pl.loop(0, w)
            def _(q):
                send_dn(c, q).wait_recv()
                total = part[lax.rem(c, 2), q] + dn_in[c, q].astype(jnp.float32)
                dn_out[c, q] = total.astype(jnp.bfloat16)
                send_dn(c, q).start()

    def relay_near_end(c):
        @pl.when(2 * w < n_pw)
        def _():
            upward(c)

        @pl.when(2 * w >= n_pw)
        def _():
            downward(c)

    def relay_rest(c):
        @pl.when(2 * w < n_pw)
        def _():
            downward(c)

        @pl.when(2 * w >= n_pw)
        def _():
            upward(c)

        final[c] = part[lax.rem(c, 2), w]

        @pl.when(w > 0)
        def _():
            send_up(c, w).wait_recv()
            final[c] += up_in[c, w].astype(jnp.float32)

        @pl.when(w < n_pw - 1)
        def _():
            send_dn(c, w).wait_recv()
            final[c] += dn_in[c, w].astype(jnp.float32)

    @pl.loop(0, chunks)
    def _(c):
        multiply(c)
        relay_near_end(c)

        @pl.when(c > 0)
        def _():
            relay_rest(c - 1)

    relay_rest(chunks - 1)

    tall = final.shape[1]

    def write(c, place):
        for f in range(own_rows // tall):
            block = final[c][:, f * 2 * rows:(f + 1) * 2 * rows]
            for h in range(2):
                s, unit = place[h]
                out_ref[s, f * tall:(f + 1) * tall, unit * rows:(unit + 1) * rows] = (
                    block[:, h * rows:(h + 1) * rows]
                )

    @pl.when(even)
    def _():
        for c in range(chunks):
            write(c, ((0, c), (1, c)))

    @pl.when(jnp.logical_not(even))
    def _():
        for c in range(chunks):
            slot, unit = c // half, 2 * (c % half)
            write(c, ((slot, unit), (slot, unit + 1)))

    send_index(0, one_on).wait_send()
    send_index(1, two_on).wait_send()

    @pl.loop(0, chunks)
    def _(c):
        send_near(c).wait_send()

        @pl.when(even)
        def _():
            send_far(c).wait_send()
            forward(c).wait_send()

        @pl.when(w < n_pw - 1)
        def _():
            @pl.loop(w + 1, n_pw)
            def _(q):
                send_up(c, q).wait_send()

        @pl.when(w > 0)
        def _():
            @pl.loop(0, w)
            def _(q):
                send_dn(c, q).wait_send()


def local(n_blk, n_pw, res_pair, band_pair, coulomb, screening, val_form, cond_form, res_bands, band_bands):
    n_res, depth = res_pair.shape
    n_band = band_pair.shape[0]
    width = val_form.shape[1]
    n_val, n_cond = val_form.shape[0], cond_form.shape[0]
    chunks = 4 if n_pw <= 4 else 2
    rows = n_band // chunks
    own_rows = n_res // n_pw
    fold = max(1, LANES // (2 * rows))
    tall, wide = own_rows // fold, 2 * rows * fold
    bf16, f32, i32 = jnp.bfloat16, jnp.float32, jnp.int32
    dma = pltpu.SemaphoreType.DMA
    vmem = pl.BlockSpec(memory_space=pltpu.VMEM)
    return pl.pallas_call(
        functools.partial(kernel, n_blk, n_pw),
        out_shape=jax.ShapeDtypeStruct((STEPS, own_rows, n_band), f32),
        in_specs=[pl.BlockSpec(memory_space=pl.ANY)] + [vmem] * 7,
        out_specs=vmem,
        scratch_shapes=[
            pltpu.VMEM((n_res, depth), bf16),
            dma(()),
            pltpu.VMEM((rounded_up(n_val, LANES), width), bf16),
            pltpu.VMEM((rounded_up(n_cond, LANES), width), bf16),
            pltpu.VMEM((n_res, width), bf16),
            pltpu.VMEM((8, n_band), i32),
            pltpu.VMEM((2, 8, n_band), i32),
            pltpu.VMEM((chunks, rows, depth), bf16),
            pltpu.VMEM((2, chunks, rows, depth), bf16),
            pltpu.VMEM((2, chunks, rows, width), bf16),
            pltpu.VMEM((2, n_pw, tall, wide), f32),
            pltpu.VMEM((chunks, n_pw, tall, wide), bf16),
            pltpu.VMEM((chunks, n_pw, tall, wide), bf16),
            pltpu.VMEM((chunks, n_pw, tall, wide), bf16),
            pltpu.VMEM((chunks, n_pw, tall, wide), bf16),
            pltpu.VMEM((chunks, tall, wide), f32),
            dma((2,)),
            dma((2,)),
            dma((chunks,)),
            dma((chunks,)),
            dma((chunks,)),
            dma((2, chunks)),
            dma((chunks, n_pw)),
            dma((chunks, n_pw)),
            dma((chunks, n_pw)),
            dma((chunks, n_pw)),
        ],
        compiler_params=pltpu.CompilerParams(
            collective_id=0, has_side_effects=True, vmem_limit_bytes=56 * 1024 * 1024
        ),
        cost_estimate=pl.CostEstimate(
            flops=2 * STEPS * n_res * n_band * (depth + width),
            bytes_accessed=2 * n_res * depth,
            transcendentals=0,
        ),
        name="kernel_blocks",
    )(res_pair, band_pair, coulomb[None, :], screening[None, :], val_form, cond_form, res_bands, band_bands)


def solution(mesh):
    return jax.shard_map(
        functools.partial(local, mesh.shape["blk"], mesh.shape["pw"]),
        mesh=mesh,
        in_specs=(
            P("blk", "pw"),
            P("blk", "pw"),
            P("pw"),
            P("pw"),
            P(None, "pw"),
            P(None, "pw"),
            P(None, "blk"),
            P(None, "blk"),
        ),
        out_specs=P(None, ("blk", "pw"), None),
        check_vma=False,
    )
```

```python
import functools

import jax
import jax.numpy as jnp
from jax import lax
from jax.experimental import pallas as pl
from jax.experimental.pallas import tpu as pltpu
from jax.sharding import PartitionSpec as P

NV = 200
NC = 300
STEPS = 2
LANES = 128
GROUP = 256
MESH = pl.DeviceIdType.MESH


def rounded_up(count, unit):
    return (count + unit - 1) // unit * unit


def kernel(
    n_blk, n_pw,
    res_hbm, band_ref, coul_ref, scr_ref, val_form, cond_form, res_bands, band_bands, out_ref,
    res, res_sem, val_pad, cond_pad, dens, bidx, idx_in, wgt, rhs, rhs_scr, part, up_in, dn_in, up_out, dn_out, final,
    idx_send, idx_recv, near_send, far_send, fwd_send, rhs_recv,
    up_send, up_recv, dn_send, dn_recv,
):
    chunks, rows = wgt.shape[0], wgt.shape[1]
    own_rows = out_ref.shape[1]
    me = lax.axis_index("blk")
    w = lax.axis_index("pw")
    even = lax.rem(me, 2) == 0
    one_on, two_on = lax.rem(me + 1, n_blk), lax.rem(me + 2, n_blk)
    one_back, two_back = lax.rem(me + n_blk - 1, n_blk), lax.rem(me + n_blk - 2, n_blk)

    load = pltpu.make_async_copy(res_hbm, res, res_sem)
    load.start()

    barrier = pltpu.get_barrier_semaphore()
    for other in (one_on, two_on, one_back, two_back):
        pl.semaphore_signal(barrier, inc=1, device_id=(other, w), device_id_type=MESH)

    @pl.when(w > 0)
    def _():
        pl.semaphore_signal(barrier, inc=1, device_id=(me, w - 1), device_id_type=MESH)

    @pl.when(w < n_pw - 1)
    def _():
        pl.semaphore_signal(barrier, inc=1, device_id=(me, w + 1), device_id_type=MESH)

    peers = 4 + jnp.where(w > 0, 1, 0) + jnp.where(w < n_pw - 1, 1, 0)
    pl.semaphore_wait(barrier, peers)

    def remote(src, dst, send, recv, blk, pw):
        return pltpu.make_async_remote_copy(
            src_ref=src, dst_ref=dst, send_sem=send, recv_sem=recv,
            device_id=(blk, pw), device_id_type=MESH,
        )

    def send_index(slot, target):
        return remote(bidx, idx_in.at[slot], idx_send.at[slot], idx_recv.at[slot], target, w)

    def send_near(c):
        return remote(wgt.at[c], rhs.at[0, c], near_send.at[c], rhs_recv.at[0, c], one_on, w)

    def send_far(c):
        return remote(wgt.at[c], rhs.at[1, c], far_send.at[c], rhs_recv.at[1, c], two_on, w)

    def forward(c):
        return remote(rhs.at[0, c], rhs.at[1, c], fwd_send.at[c], rhs_recv.at[1, c], one_on, w)

    def send_up(c, q):
        return remote(up_out.at[c, q], up_in.at[c, q], up_send.at[c, q], up_recv.at[c, q], me, w + 1)

    def send_dn(c, q):
        return remote(dn_out.at[c, q], dn_in.at[c, q], dn_send.at[c, q], dn_recv.at[c, q], me, w - 1)

    bidx[...] = jnp.zeros_like(bidx)
    bidx[0:1, :] = band_bands[2:3, :] * NV + band_bands[0:1, :]
    bidx[1:2, :] = band_bands[2:3, :] * NC + band_bands[1:2, :]
    send_index(0, one_on).start()
    send_index(1, two_on).start()

    @pl.loop(0, chunks)
    def _(c):
        block = band_ref[pl.ds(pl.multiple_of(c * rows, rows), rows), :].astype(jnp.float32)
        wgt[c] = (block * (2.0 * coul_ref[...])).astype(jnp.bfloat16)
        send_near(c).start()

        @pl.when(even)
        def _():
            send_far(c).start()

    for form, padded in ((val_form, val_pad), (cond_form, cond_pad)):
        spare = jnp.zeros((padded.shape[0] - form.shape[0], form.shape[1]), jnp.float32)
        padded[...] = jnp.concatenate([form[...].astype(jnp.float32), spare], axis=0).astype(padded.dtype)

    def one_hot(row, depth):
        column = jnp.concatenate(
            [
                jnp.broadcast_to(row[:, h * LANES:(h + 1) * LANES], (LANES, LANES)).T
                for h in range(GROUP // LANES)
            ],
            axis=0,
        )
        lane = lax.broadcasted_iota(jnp.int32, (GROUP, LANES), 1)
        return jnp.concatenate(
            [
                jnp.where(column == lane + start, 1.0, 0.0).astype(jnp.bfloat16)
                for start in range(0, depth, LANES)
            ],
            axis=1,
        )

    def density(val_row, cond_row):
        valence = jnp.dot(
            one_hot(val_row, val_pad.shape[0]), val_pad[...], preferred_element_type=jnp.float32
        )
        conduct = jnp.dot(
            one_hot(cond_row, cond_pad.shape[0]), cond_pad[...], preferred_element_type=jnp.float32
        )
        return (valence * conduct).astype(jnp.bfloat16)

    @pl.loop(0, dens.shape[0] // GROUP)
    def _(g):
        at = pl.ds(pl.multiple_of(g * GROUP, GROUP), GROUP)
        point = res_bands[2:3, at]
        dens[at, :] = density(point * NV + res_bands[0:1, at], point * NC + res_bands[1:2, at])

    for slot, target in ((0, one_on), (1, two_on)):
        send_index(slot, target).wait_recv()
        for g in range(chunks * rows // GROUP):
            at = slice(g * GROUP, (g + 1) * GROUP)
            block = density(idx_in[slot, 0:1, at], idx_in[slot, 1:2, at])
            block = (block.astype(jnp.float32) * (-scr_ref[...])).astype(jnp.bfloat16)
            for h in range(GROUP // rows):
                rhs_scr[slot, g * (GROUP // rows) + h] = block[h * rows:(h + 1) * rows, :]

    load.wait()

    half = chunks // 2

    def parts_of(c):
        slot, unit = c // half, 2 * (c % half)
        return (
            (jnp.where(even, 0, slot), jnp.where(even, c, unit)),
            (jnp.where(even, 1, slot), jnp.where(even, c, unit + 1)),
        )

    def landed(slot, unit):
        remote(wgt.at[0], rhs.at[slot, unit], near_send.at[0], rhs_recv.at[slot, unit], one_on, w).wait_recv()

    def packed(term):
        if 2 * rows >= LANES:
            return term
        fold = LANES // (2 * rows)
        tall = own_rows // fold
        return jnp.concatenate([term[f * tall:(f + 1) * tall] for f in range(fold)], axis=1)

    def multiply(c):
        first, second = parts_of(c)
        landed(*first)

        @pl.when(even)
        def _():
            forward(c).start()

        landed(*second)
        weighted = jnp.concatenate([rhs[first], rhs[second]], axis=0)
        screened = jnp.concatenate([rhs_scr[first], rhs_scr[second]], axis=0)

        @pl.loop(0, n_pw)
        def _(j):
            q = jnp.where(2 * w < n_pw, n_pw - 1 - j, j)
            at = pl.ds(pl.multiple_of(q * own_rows, own_rows), own_rows)
            contract = (((1,), (1,)), ((), ()))
            term = lax.dot_general(
                res[at, :], weighted, contract, preferred_element_type=jnp.float32
            ) + lax.dot_general(
                dens[at, :], screened, contract, preferred_element_type=jnp.float32
            )
            term = packed(term)
            part[lax.rem(c, 2), q] = term

            @pl.when(jnp.logical_and(w == 0, q > 0))
            def _():
                up_out[c, q] = term.astype(jnp.bfloat16)
                send_up(c, q).start()

            @pl.when(jnp.logical_and(w == n_pw - 1, q < n_pw - 1))
            def _():
                dn_out[c, q] = term.astype(jnp.bfloat16)
                send_dn(c, q).start()

    def upward(c):
        @pl.when(w > 0)
        def _():
            @pl.loop(0, n_pw - 1 - w)
            def _(j):
                q = n_pw - 1 - j
                send_up(c, q).wait_recv()
                total = part[lax.rem(c, 2), q] + up_in[c, q].astype(jnp.float32)
                up_out[c, q] = total.astype(jnp.bfloat16)
                send_up(c, q).start()

    def downward(c):
        @pl.when(w < n_pw - 1)
        def _():
            @pl.loop(0, w)
            def _(q):
                send_dn(c, q).wait_recv()
                total = part[lax.rem(c, 2), q] + dn_in[c, q].astype(jnp.float32)
                dn_out[c, q] = total.astype(jnp.bfloat16)
                send_dn(c, q).start()

    def relay_near_end(c):
        @pl.when(2 * w < n_pw)
        def _():
            upward(c)

        @pl.when(2 * w >= n_pw)
        def _():
            downward(c)

    def relay_rest(c):
        @pl.when(2 * w < n_pw)
        def _():
            downward(c)

        @pl.when(2 * w >= n_pw)
        def _():
            upward(c)

        final[c] = part[lax.rem(c, 2), w]

        @pl.when(w > 0)
        def _():
            send_up(c, w).wait_recv()
            final[c] += up_in[c, w].astype(jnp.float32)

        @pl.when(w < n_pw - 1)
        def _():
            send_dn(c, w).wait_recv()
            final[c] += dn_in[c, w].astype(jnp.float32)

    @pl.loop(0, chunks)
    def _(c):
        multiply(c)
        relay_near_end(c)

        @pl.when(c > 0)
        def _():
            relay_rest(c - 1)

    relay_rest(chunks - 1)

    tall = final.shape[1]

    def write(c, place):
        for f in range(own_rows // tall):
            block = final[c][:, f * 2 * rows:(f + 1) * 2 * rows]
            for h in range(2):
                s, unit = place[h]
                out_ref[s, f * tall:(f + 1) * tall, unit * rows:(unit + 1) * rows] = (
                    block[:, h * rows:(h + 1) * rows]
                )

    @pl.when(even)
    def _():
        for c in range(chunks):
            write(c, ((0, c), (1, c)))

    @pl.when(jnp.logical_not(even))
    def _():
        for c in range(chunks):
            slot, unit = c // half, 2 * (c % half)
            write(c, ((slot, unit), (slot, unit + 1)))

    send_index(0, one_on).wait_send()
    send_index(1, two_on).wait_send()

    @pl.loop(0, chunks)
    def _(c):
        send_near(c).wait_send()

        @pl.when(even)
        def _():
            send_far(c).wait_send()
            forward(c).wait_send()

        @pl.when(w < n_pw - 1)
        def _():
            @pl.loop(w + 1, n_pw)
            def _(q):
                send_up(c, q).wait_send()

        @pl.when(w > 0)
        def _():
            @pl.loop(0, w)
            def _(q):
                send_dn(c, q).wait_send()


def local(n_blk, n_pw, res_pair, band_pair, coulomb, screening, val_form, cond_form, res_bands, band_bands):
    n_res, depth = res_pair.shape
    n_band = band_pair.shape[0]
    width = val_form.shape[1]
    n_val, n_cond = val_form.shape[0], cond_form.shape[0]
    chunks = 8 if n_pw <= 4 else 2
    rows = n_band // chunks
    own_rows = n_res // n_pw
    fold = max(1, LANES // (2 * rows))
    tall, wide = own_rows // fold, 2 * rows * fold
    bf16, f32, i32 = jnp.bfloat16, jnp.float32, jnp.int32
    dma = pltpu.SemaphoreType.DMA
    vmem = pl.BlockSpec(memory_space=pltpu.VMEM)
    return pl.pallas_call(
        functools.partial(kernel, n_blk, n_pw),
        out_shape=jax.ShapeDtypeStruct((STEPS, own_rows, n_band), f32),
        in_specs=[pl.BlockSpec(memory_space=pl.ANY)] + [vmem] * 7,
        out_specs=vmem,
        scratch_shapes=[
            pltpu.VMEM((n_res, depth), bf16),
            dma(()),
            pltpu.VMEM((rounded_up(n_val, LANES), width), bf16),
            pltpu.VMEM((rounded_up(n_cond, LANES), width), bf16),
            pltpu.VMEM((n_res, width), bf16),
            pltpu.VMEM((8, n_band), i32),
            pltpu.VMEM((2, 8, n_band), i32),
            pltpu.VMEM((chunks, rows, depth), bf16),
            pltpu.VMEM((2, chunks, rows, depth), bf16),
            pltpu.VMEM((2, chunks, rows, width), bf16),
            pltpu.VMEM((2, n_pw, tall, wide), f32),
            pltpu.VMEM((chunks, n_pw, tall, wide), bf16),
            pltpu.VMEM((chunks, n_pw, tall, wide), bf16),
            pltpu.VMEM((chunks, n_pw, tall, wide), bf16),
            pltpu.VMEM((chunks, n_pw, tall, wide), bf16),
            pltpu.VMEM((chunks, tall, wide), f32),
            dma((2,)),
            dma((2,)),
            dma((chunks,)),
            dma((chunks,)),
            dma((chunks,)),
            dma((2, chunks)),
            dma((chunks, n_pw)),
            dma((chunks, n_pw)),
            dma((chunks, n_pw)),
            dma((chunks, n_pw)),
        ],
        compiler_params=pltpu.CompilerParams(
            collective_id=0, has_side_effects=True, vmem_limit_bytes=56 * 1024 * 1024
        ),
        cost_estimate=pl.CostEstimate(
            flops=2 * STEPS * n_res * n_band * (depth + width),
            bytes_accessed=2 * n_res * depth,
            transcendentals=0,
        ),
        name="kernel_blocks",
    )(res_pair, band_pair, coulomb[None, :], screening[None, :], val_form, cond_form, res_bands, band_bands)


def solution(mesh):
    return jax.shard_map(
        functools.partial(local, mesh.shape["blk"], mesh.shape["pw"]),
        mesh=mesh,
        in_specs=(
            P("blk", "pw"),
            P("blk", "pw"),
            P("pw"),
            P("pw"),
            P(None, "pw"),
            P(None, "pw"),
            P(None, "blk"),
            P(None, "blk"),
        ),
        out_specs=P(None, ("blk", "pw"), None),
        check_vma=False,
    )
```

```python
import functools

import jax
import jax.numpy as jnp
from jax import lax
from jax.experimental import pallas as pl
from jax.experimental.pallas import tpu as pltpu
from jax.sharding import PartitionSpec as P

NV = 200
NC = 300
STEPS = 2
LANES = 128
GROUP = 256
MESH = pl.DeviceIdType.MESH


def rounded_up(count, unit):
    return (count + unit - 1) // unit * unit


def kernel(
    n_blk, n_pw,
    res_hbm, band_ref, coul_ref, scr_ref, val_form, cond_form, res_bands, band_bands, out_ref,
    res, res_sem, val_pad, cond_pad, dens, bidx, idx_in, wgt, rhs, rhs_scr, turned, part, up_in, dn_in, up_out, dn_out, final,
    idx_send, idx_recv, near_send, far_send, fwd_send, rhs_recv,
    up_send, up_recv, dn_send, dn_recv,
):
    chunks, rows = wgt.shape[0], wgt.shape[1]
    own_rows = out_ref.shape[1]
    me = lax.axis_index("blk")
    w = lax.axis_index("pw")
    even = lax.rem(me, 2) == 0
    one_on, two_on = lax.rem(me + 1, n_blk), lax.rem(me + 2, n_blk)
    one_back, two_back = lax.rem(me + n_blk - 1, n_blk), lax.rem(me + n_blk - 2, n_blk)

    load = pltpu.make_async_copy(res_hbm, res, res_sem)
    load.start()

    barrier = pltpu.get_barrier_semaphore()
    for other in (one_on, two_on, one_back, two_back):
        pl.semaphore_signal(barrier, inc=1, device_id=(other, w), device_id_type=MESH)

    @pl.when(w > 0)
    def _():
        pl.semaphore_signal(barrier, inc=1, device_id=(me, w - 1), device_id_type=MESH)

    @pl.when(w < n_pw - 1)
    def _():
        pl.semaphore_signal(barrier, inc=1, device_id=(me, w + 1), device_id_type=MESH)

    peers = 4 + jnp.where(w > 0, 1, 0) + jnp.where(w < n_pw - 1, 1, 0)
    pl.semaphore_wait(barrier, peers)

    def remote(src, dst, send, recv, blk, pw):
        return pltpu.make_async_remote_copy(
            src_ref=src, dst_ref=dst, send_sem=send, recv_sem=recv,
            device_id=(blk, pw), device_id_type=MESH,
        )

    def send_index(slot, target):
        return remote(bidx, idx_in.at[slot], idx_send.at[slot], idx_recv.at[slot], target, w)

    def send_near(c):
        return remote(wgt.at[c], rhs.at[0, c], near_send.at[c], rhs_recv.at[0, c], one_on, w)

    def send_far(c):
        return remote(wgt.at[c], rhs.at[1, c], far_send.at[c], rhs_recv.at[1, c], two_on, w)

    def forward(c):
        return remote(rhs.at[0, c], rhs.at[1, c], fwd_send.at[c], rhs_recv.at[1, c], one_on, w)

    def send_up(c, q):
        return remote(up_out.at[c, q], up_in.at[c, q], up_send.at[c, q], up_recv.at[c, q], me, w + 1)

    def send_dn(c, q):
        return remote(dn_out.at[c, q], dn_in.at[c, q], dn_send.at[c, q], dn_recv.at[c, q], me, w - 1)

    bidx[...] = jnp.zeros_like(bidx)
    bidx[0:1, :] = band_bands[2:3, :] * NV + band_bands[0:1, :]
    bidx[1:2, :] = band_bands[2:3, :] * NC + band_bands[1:2, :]
    send_index(0, one_on).start()
    send_index(1, two_on).start()

    @pl.loop(0, chunks)
    def _(c):
        block = band_ref[pl.ds(pl.multiple_of(c * rows, rows), rows), :].astype(jnp.float32)
        wgt[c] = (block * (2.0 * coul_ref[...])).astype(jnp.bfloat16)
        send_near(c).start()

        @pl.when(even)
        def _():
            send_far(c).start()

    for form, padded in ((val_form, val_pad), (cond_form, cond_pad)):
        spare = jnp.zeros((padded.shape[0] - form.shape[0], form.shape[1]), jnp.float32)
        padded[...] = jnp.concatenate([form[...].astype(jnp.float32), spare], axis=0).astype(padded.dtype)

    def one_hot(row, depth):
        column = jnp.concatenate(
            [
                jnp.broadcast_to(row[:, h * LANES:(h + 1) * LANES], (LANES, LANES)).T
                for h in range(GROUP // LANES)
            ],
            axis=0,
        )
        lane = lax.broadcasted_iota(jnp.int32, (GROUP, LANES), 1)
        return jnp.concatenate(
            [
                jnp.where(column == lane + start, 1.0, 0.0).astype(jnp.bfloat16)
                for start in range(0, depth, LANES)
            ],
            axis=1,
        )

    def density(val_row, cond_row):
        valence = jnp.dot(
            one_hot(val_row, val_pad.shape[0]), val_pad[...], preferred_element_type=jnp.float32
        )
        conduct = jnp.dot(
            one_hot(cond_row, cond_pad.shape[0]), cond_pad[...], preferred_element_type=jnp.float32
        )
        return (valence * conduct).astype(jnp.bfloat16)

    @pl.loop(0, dens.shape[0] // GROUP)
    def _(g):
        at = pl.ds(pl.multiple_of(g * GROUP, GROUP), GROUP)
        point = res_bands[2:3, at]
        dens[at, :] = density(point * NV + res_bands[0:1, at], point * NC + res_bands[1:2, at])

    for slot, target in ((0, one_on), (1, two_on)):
        send_index(slot, target).wait_recv()
        for g in range(chunks * rows // GROUP):
            at = slice(g * GROUP, (g + 1) * GROUP)
            block = density(idx_in[slot, 0:1, at], idx_in[slot, 1:2, at])
            block = (block.astype(jnp.float32) * (-scr_ref[...])).astype(jnp.bfloat16)
            for h in range(GROUP // rows):
                rhs_scr[slot, g * (GROUP // rows) + h] = block[h * rows:(h + 1) * rows, :]

    load.wait()

    half = chunks // 2

    def parts_of(c):
        slot, unit = c // half, 2 * (c % half)
        return (
            (jnp.where(even, 0, slot), jnp.where(even, c, unit)),
            (jnp.where(even, 1, slot), jnp.where(even, c, unit + 1)),
        )

    def landed(slot, unit):
        remote(wgt.at[0], rhs.at[slot, unit], near_send.at[0], rhs_recv.at[slot, unit], one_on, w).wait_recv()

    def packed(term):
        if 2 * rows >= LANES:
            return term
        fold = LANES // (2 * rows)
        tall = own_rows // fold
        return jnp.concatenate([term[f * tall:(f + 1) * tall] for f in range(fold)], axis=1)

    def multiply(c):
        first, second = parts_of(c)
        landed(*first)

        @pl.when(even)
        def _():
            forward(c).start()

        landed(*second)
        depth = rhs.shape[3]
        turned[:depth, :] = jnp.concatenate([rhs[first], rhs[second]], axis=0).T
        turned[depth:, :] = jnp.concatenate([rhs_scr[first], rhs_scr[second]], axis=0).T

        @pl.loop(0, n_pw)
        def _(j):
            q = jnp.where(2 * w < n_pw, n_pw - 1 - j, j)
            at = pl.ds(pl.multiple_of(q * own_rows, own_rows), own_rows)
            term = jnp.dot(
                res[at, :], turned[:depth, :], preferred_element_type=jnp.float32
            ) + jnp.dot(dens[at, :], turned[depth:, :], preferred_element_type=jnp.float32)
            term = packed(term)
            part[lax.rem(c, 2), q] = term

            @pl.when(jnp.logical_and(w == 0, q > 0))
            def _():
                up_out[c, q] = term.astype(jnp.bfloat16)
                send_up(c, q).start()

            @pl.when(jnp.logical_and(w == n_pw - 1, q < n_pw - 1))
            def _():
                dn_out[c, q] = term.astype(jnp.bfloat16)
                send_dn(c, q).start()

    def upward(c):
        @pl.when(w > 0)
        def _():
            @pl.loop(0, n_pw - 1 - w)
            def _(j):
                q = n_pw - 1 - j
                send_up(c, q).wait_recv()
                total = part[lax.rem(c, 2), q] + up_in[c, q].astype(jnp.float32)
                up_out[c, q] = total.astype(jnp.bfloat16)
                send_up(c, q).start()

    def downward(c):
        @pl.when(w < n_pw - 1)
        def _():
            @pl.loop(0, w)
            def _(q):
                send_dn(c, q).wait_recv()
                total = part[lax.rem(c, 2), q] + dn_in[c, q].astype(jnp.float32)
                dn_out[c, q] = total.astype(jnp.bfloat16)
                send_dn(c, q).start()

    def relay_near_end(c):
        @pl.when(2 * w < n_pw)
        def _():
            upward(c)

        @pl.when(2 * w >= n_pw)
        def _():
            downward(c)

    def relay_rest(c):
        @pl.when(2 * w < n_pw)
        def _():
            downward(c)

        @pl.when(2 * w >= n_pw)
        def _():
            upward(c)

        final[c] = part[lax.rem(c, 2), w]

        @pl.when(w > 0)
        def _():
            send_up(c, w).wait_recv()
            final[c] += up_in[c, w].astype(jnp.float32)

        @pl.when(w < n_pw - 1)
        def _():
            send_dn(c, w).wait_recv()
            final[c] += dn_in[c, w].astype(jnp.float32)

    @pl.loop(0, chunks)
    def _(c):
        multiply(c)
        relay_near_end(c)

        @pl.when(c > 0)
        def _():
            relay_rest(c - 1)

    relay_rest(chunks - 1)

    tall = final.shape[1]

    def write(c, place):
        for f in range(own_rows // tall):
            block = final[c][:, f * 2 * rows:(f + 1) * 2 * rows]
            for h in range(2):
                s, unit = place[h]
                out_ref[s, f * tall:(f + 1) * tall, unit * rows:(unit + 1) * rows] = (
                    block[:, h * rows:(h + 1) * rows]
                )

    @pl.when(even)
    def _():
        for c in range(chunks):
            write(c, ((0, c), (1, c)))

    @pl.when(jnp.logical_not(even))
    def _():
        for c in range(chunks):
            slot, unit = c // half, 2 * (c % half)
            write(c, ((slot, unit), (slot, unit + 1)))

    send_index(0, one_on).wait_send()
    send_index(1, two_on).wait_send()

    @pl.loop(0, chunks)
    def _(c):
        send_near(c).wait_send()

        @pl.when(even)
        def _():
            send_far(c).wait_send()
            forward(c).wait_send()

        @pl.when(w < n_pw - 1)
        def _():
            @pl.loop(w + 1, n_pw)
            def _(q):
                send_up(c, q).wait_send()

        @pl.when(w > 0)
        def _():
            @pl.loop(0, w)
            def _(q):
                send_dn(c, q).wait_send()


def local(n_blk, n_pw, res_pair, band_pair, coulomb, screening, val_form, cond_form, res_bands, band_bands):
    n_res, depth = res_pair.shape
    n_band = band_pair.shape[0]
    width = val_form.shape[1]
    n_val, n_cond = val_form.shape[0], cond_form.shape[0]
    chunks = 4 if n_pw <= 4 else 2
    rows = n_band // chunks
    own_rows = n_res // n_pw
    fold = max(1, LANES // (2 * rows))
    tall, wide = own_rows // fold, 2 * rows * fold
    bf16, f32, i32 = jnp.bfloat16, jnp.float32, jnp.int32
    dma = pltpu.SemaphoreType.DMA
    vmem = pl.BlockSpec(memory_space=pltpu.VMEM)
    return pl.pallas_call(
        functools.partial(kernel, n_blk, n_pw),
        out_shape=jax.ShapeDtypeStruct((STEPS, own_rows, n_band), f32),
        in_specs=[pl.BlockSpec(memory_space=pl.ANY)] + [vmem] * 7,
        out_specs=vmem,
        scratch_shapes=[
            pltpu.VMEM((n_res, depth), bf16),
            dma(()),
            pltpu.VMEM((rounded_up(n_val, LANES), width), bf16),
            pltpu.VMEM((rounded_up(n_cond, LANES), width), bf16),
            pltpu.VMEM((n_res, width), bf16),
            pltpu.VMEM((8, n_band), i32),
            pltpu.VMEM((2, 8, n_band), i32),
            pltpu.VMEM((chunks, rows, depth), bf16),
            pltpu.VMEM((2, chunks, rows, depth), bf16),
            pltpu.VMEM((2, chunks, rows, width), bf16),
            pltpu.VMEM((depth + width, 2 * rows), bf16),
            pltpu.VMEM((2, n_pw, tall, wide), f32),
            pltpu.VMEM((chunks, n_pw, tall, wide), bf16),
            pltpu.VMEM((chunks, n_pw, tall, wide), bf16),
            pltpu.VMEM((chunks, n_pw, tall, wide), bf16),
            pltpu.VMEM((chunks, n_pw, tall, wide), bf16),
            pltpu.VMEM((chunks, tall, wide), f32),
            dma((2,)),
            dma((2,)),
            dma((chunks,)),
            dma((chunks,)),
            dma((chunks,)),
            dma((2, chunks)),
            dma((chunks, n_pw)),
            dma((chunks, n_pw)),
            dma((chunks, n_pw)),
            dma((chunks, n_pw)),
        ],
        compiler_params=pltpu.CompilerParams(
            collective_id=0, has_side_effects=True, vmem_limit_bytes=56 * 1024 * 1024
        ),
        cost_estimate=pl.CostEstimate(
            flops=2 * STEPS * n_res * n_band * (depth + width),
            bytes_accessed=2 * n_res * depth,
            transcendentals=0,
        ),
        name="kernel_blocks",
    )(res_pair, band_pair, coulomb[None, :], screening[None, :], val_form, cond_form, res_bands, band_bands)


def solution(mesh):
    return jax.shard_map(
        functools.partial(local, mesh.shape["blk"], mesh.shape["pw"]),
        mesh=mesh,
        in_specs=(
            P("blk", "pw"),
            P("blk", "pw"),
            P("pw"),
            P("pw"),
            P(None, "pw"),
            P(None, "pw"),
            P(None, "blk"),
            P(None, "blk"),
        ),
        out_specs=P(None, ("blk", "pw"), None),
        check_vma=False,
    )
```

```python
import functools

import jax
import jax.numpy as jnp
from jax import lax
from jax.experimental import pallas as pl
from jax.experimental.pallas import tpu as pltpu
from jax.sharding import PartitionSpec as P

NV = 200
NC = 300
STEPS = 2
LANES = 128
GROUP = 256
MESH = pl.DeviceIdType.MESH


def rounded_up(count, unit):
    return (count + unit - 1) // unit * unit


def kernel(
    n_blk, n_pw,
    res_hbm, band_ref, coul_ref, scr_ref, val_form, cond_form, res_bands, band_bands, out_ref,
    res, res_sem, val_pad, cond_pad, dens, bidx, idx_in, wgt, rhs, rhs_scr, part, up_in, dn_in, up_out, dn_out, final,
    idx_send, idx_recv, near_send, far_send, fwd_send, rhs_recv,
    up_send, up_recv, dn_send, dn_recv,
):
    chunks, rows = wgt.shape[0], wgt.shape[1]
    own_rows = out_ref.shape[1]
    me = lax.axis_index("blk")
    w = lax.axis_index("pw")
    even = lax.rem(me, 2) == 0
    one_on, two_on = lax.rem(me + 1, n_blk), lax.rem(me + 2, n_blk)
    one_back, two_back = lax.rem(me + n_blk - 1, n_blk), lax.rem(me + n_blk - 2, n_blk)

    load = pltpu.make_async_copy(res_hbm, res, res_sem)
    load.start()

    barrier = pltpu.get_barrier_semaphore()
    for other in (one_on, two_on, one_back, two_back):
        pl.semaphore_signal(barrier, inc=1, device_id=(other, w), device_id_type=MESH)

    @pl.when(w > 0)
    def _():
        pl.semaphore_signal(barrier, inc=1, device_id=(me, w - 1), device_id_type=MESH)

    @pl.when(w < n_pw - 1)
    def _():
        pl.semaphore_signal(barrier, inc=1, device_id=(me, w + 1), device_id_type=MESH)

    peers = 4 + jnp.where(w > 0, 1, 0) + jnp.where(w < n_pw - 1, 1, 0)
    pl.semaphore_wait(barrier, peers)

    def remote(src, dst, send, recv, blk, pw):
        return pltpu.make_async_remote_copy(
            src_ref=src, dst_ref=dst, send_sem=send, recv_sem=recv,
            device_id=(blk, pw), device_id_type=MESH,
        )

    def send_index(slot, target):
        return remote(bidx, idx_in.at[slot], idx_send.at[slot], idx_recv.at[slot], target, w)

    def send_near(c):
        return remote(wgt.at[c], rhs.at[0, c], near_send.at[c], rhs_recv.at[0, c], one_on, w)

    def send_far(c):
        return remote(wgt.at[c], rhs.at[1, c], far_send.at[c], rhs_recv.at[1, c], two_on, w)

    def forward(c):
        return remote(rhs.at[0, c], rhs.at[1, c], fwd_send.at[c], rhs_recv.at[1, c], one_on, w)

    def send_up(c, q):
        return remote(up_out.at[c, q], up_in.at[c, q], up_send.at[c, q], up_recv.at[c, q], me, w + 1)

    def send_dn(c, q):
        return remote(dn_out.at[c, q], dn_in.at[c, q], dn_send.at[c, q], dn_recv.at[c, q], me, w - 1)

    bidx[...] = jnp.zeros_like(bidx)
    bidx[0:1, :] = band_bands[2:3, :] * NV + band_bands[0:1, :]
    bidx[1:2, :] = band_bands[2:3, :] * NC + band_bands[1:2, :]
    send_index(0, one_on).start()
    send_index(1, two_on).start()

    @pl.loop(0, chunks)
    def _(c):
        block = band_ref[pl.ds(pl.multiple_of(c * rows, rows), rows), :].astype(jnp.float32)
        wgt[c] = (block * (2.0 * coul_ref[...])).astype(jnp.bfloat16)
        send_near(c).start()

        @pl.when(even)
        def _():
            send_far(c).start()

    for form, padded in ((val_form, val_pad), (cond_form, cond_pad)):
        spare = jnp.zeros((padded.shape[0] - form.shape[0], form.shape[1]), jnp.float32)
        padded[...] = jnp.concatenate([form[...].astype(jnp.float32), spare], axis=0).astype(padded.dtype)

    def one_hot(row, depth):
        column = jnp.concatenate(
            [
                jnp.broadcast_to(row[:, h * LANES:(h + 1) * LANES], (LANES, LANES)).T
                for h in range(GROUP // LANES)
            ],
            axis=0,
        )
        lane = lax.broadcasted_iota(jnp.int32, (GROUP, LANES), 1)
        return jnp.concatenate(
            [
                jnp.where(column == lane + start, 1.0, 0.0).astype(jnp.bfloat16)
                for start in range(0, depth, LANES)
            ],
            axis=1,
        )

    def density(val_row, cond_row):
        valence = jnp.dot(
            one_hot(val_row, val_pad.shape[0]), val_pad[...], preferred_element_type=jnp.float32
        )
        conduct = jnp.dot(
            one_hot(cond_row, cond_pad.shape[0]), cond_pad[...], preferred_element_type=jnp.float32
        )
        return (valence * conduct).astype(jnp.bfloat16)

    @pl.loop(0, dens.shape[0] // GROUP)
    def _(g):
        at = pl.ds(pl.multiple_of(g * GROUP, GROUP), GROUP)
        point = res_bands[2:3, at]
        dens[at, :] = density(point * NV + res_bands[0:1, at], point * NC + res_bands[1:2, at])

    for slot, target in ((0, one_on), (1, two_on)):
        send_index(slot, target).wait_recv()
        for g in range(chunks * rows // GROUP):
            at = slice(g * GROUP, (g + 1) * GROUP)
            block = density(idx_in[slot, 0:1, at], idx_in[slot, 1:2, at])
            block = (block.astype(jnp.float32) * (-scr_ref[...])).astype(jnp.bfloat16)
            for h in range(GROUP // rows):
                rhs_scr[slot, g * (GROUP // rows) + h] = block[h * rows:(h + 1) * rows, :]

    load.wait()

    half = chunks // 2

    def parts_of(c):
        slot, unit = c // half, 2 * (c % half)
        return (
            (jnp.where(even, 0, slot), jnp.where(even, c, unit)),
            (jnp.where(even, 1, slot), jnp.where(even, c, unit + 1)),
        )

    def landed(slot, unit):
        remote(wgt.at[0], rhs.at[slot, unit], near_send.at[0], rhs_recv.at[slot, unit], one_on, w).wait_recv()

    def packed(term):
        if 2 * rows >= LANES:
            return term
        fold = LANES // (2 * rows)
        tall = own_rows // fold
        return jnp.concatenate([term[f * tall:(f + 1) * tall] for f in range(fold)], axis=1)

    def multiply(group):
        places = []
        for c in group:
            first, second = parts_of(c)
            landed(*first)

            @pl.when(even)
            def _():
                forward(c).start()

            landed(*second)
            places += [first, second]
        weighted = jnp.concatenate([rhs[place] for place in places], axis=0)
        screened = jnp.concatenate([rhs_scr[place] for place in places], axis=0)

        @pl.loop(0, n_pw)
        def _(j):
            q = jnp.where(2 * w < n_pw, n_pw - 1 - j, j)
            at = pl.ds(pl.multiple_of(q * own_rows, own_rows), own_rows)
            contract = (((1,), (1,)), ((), ()))
            term = lax.dot_general(
                res[at, :], weighted, contract, preferred_element_type=jnp.float32
            ) + lax.dot_general(
                dens[at, :], screened, contract, preferred_element_type=jnp.float32
            )
            terms = [
                packed(term[:, k * 2 * rows:(k + 1) * 2 * rows]) for k in range(len(group))
            ]
            for c, piece in zip(group, terms):
                part[c, q] = piece

            @pl.when(jnp.logical_and(w == 0, q > 0))
            def _():
                for c, piece in zip(group, terms):
                    up_out[c, q] = piece.astype(jnp.bfloat16)
                    send_up(c, q).start()

            @pl.when(jnp.logical_and(w == n_pw - 1, q < n_pw - 1))
            def _():
                for c, piece in zip(group, terms):
                    dn_out[c, q] = piece.astype(jnp.bfloat16)
                    send_dn(c, q).start()

    def upward(c):
        @pl.when(w > 0)
        def _():
            @pl.loop(0, n_pw - 1 - w)
            def _(j):
                q = n_pw - 1 - j
                send_up(c, q).wait_recv()
                total = part[c, q] + up_in[c, q].astype(jnp.float32)
                up_out[c, q] = total.astype(jnp.bfloat16)
                send_up(c, q).start()

    def downward(c):
        @pl.when(w < n_pw - 1)
        def _():
            @pl.loop(0, w)
            def _(q):
                send_dn(c, q).wait_recv()
                total = part[c, q] + dn_in[c, q].astype(jnp.float32)
                dn_out[c, q] = total.astype(jnp.bfloat16)
                send_dn(c, q).start()

    def relay_near_end(c):
        @pl.when(2 * w < n_pw)
        def _():
            upward(c)

        @pl.when(2 * w >= n_pw)
        def _():
            downward(c)

    def relay_rest(c):
        @pl.when(2 * w < n_pw)
        def _():
            downward(c)

        @pl.when(2 * w >= n_pw)
        def _():
            upward(c)

        final[c] = part[c, w]

        @pl.when(w > 0)
        def _():
            send_up(c, w).wait_recv()
            final[c] += up_in[c, w].astype(jnp.float32)

        @pl.when(w < n_pw - 1)
        def _():
            send_dn(c, w).wait_recv()
            final[c] += dn_in[c, w].astype(jnp.float32)

    groups = [(0, 1)] + [(c,) for c in range(2, chunks)]
    late = []
    for group in groups:
        multiply(group)
        for c in group:
            relay_near_end(c)
        for c in late:
            relay_rest(c)
        late = group
    for c in late:
        relay_rest(c)

    tall = final.shape[1]

    def write(c, place):
        for f in range(own_rows // tall):
            block = final[c][:, f * 2 * rows:(f + 1) * 2 * rows]
            for h in range(2):
                s, unit = place[h]
                out_ref[s, f * tall:(f + 1) * tall, unit * rows:(unit + 1) * rows] = (
                    block[:, h * rows:(h + 1) * rows]
                )

    @pl.when(even)
    def _():
        for c in range(chunks):
            write(c, ((0, c), (1, c)))

    @pl.when(jnp.logical_not(even))
    def _():
        for c in range(chunks):
            slot, unit = c // half, 2 * (c % half)
            write(c, ((slot, unit), (slot, unit + 1)))

    send_index(0, one_on).wait_send()
    send_index(1, two_on).wait_send()

    @pl.loop(0, chunks)
    def _(c):
        send_near(c).wait_send()

        @pl.when(even)
        def _():
            send_far(c).wait_send()
            forward(c).wait_send()

        @pl.when(w < n_pw - 1)
        def _():
            @pl.loop(w + 1, n_pw)
            def _(q):
                send_up(c, q).wait_send()

        @pl.when(w > 0)
        def _():
            @pl.loop(0, w)
            def _(q):
                send_dn(c, q).wait_send()


def local(n_blk, n_pw, res_pair, band_pair, coulomb, screening, val_form, cond_form, res_bands, band_bands):
    n_res, depth = res_pair.shape
    n_band = band_pair.shape[0]
    width = val_form.shape[1]
    n_val, n_cond = val_form.shape[0], cond_form.shape[0]
    chunks = 4 if n_pw <= 4 else 2
    rows = n_band // chunks
    own_rows = n_res // n_pw
    fold = max(1, LANES // (2 * rows))
    tall, wide = own_rows // fold, 2 * rows * fold
    bf16, f32, i32 = jnp.bfloat16, jnp.float32, jnp.int32
    dma = pltpu.SemaphoreType.DMA
    vmem = pl.BlockSpec(memory_space=pltpu.VMEM)
    return pl.pallas_call(
        functools.partial(kernel, n_blk, n_pw),
        out_shape=jax.ShapeDtypeStruct((STEPS, own_rows, n_band), f32),
        in_specs=[pl.BlockSpec(memory_space=pl.ANY)] + [vmem] * 7,
        out_specs=vmem,
        scratch_shapes=[
            pltpu.VMEM((n_res, depth), bf16),
            dma(()),
            pltpu.VMEM((rounded_up(n_val, LANES), width), bf16),
            pltpu.VMEM((rounded_up(n_cond, LANES), width), bf16),
            pltpu.VMEM((n_res, width), bf16),
            pltpu.VMEM((8, n_band), i32),
            pltpu.VMEM((2, 8, n_band), i32),
            pltpu.VMEM((chunks, rows, depth), bf16),
            pltpu.VMEM((2, chunks, rows, depth), bf16),
            pltpu.VMEM((2, chunks, rows, width), bf16),
            pltpu.VMEM((chunks, n_pw, tall, wide), f32),
            pltpu.VMEM((chunks, n_pw, tall, wide), bf16),
            pltpu.VMEM((chunks, n_pw, tall, wide), bf16),
            pltpu.VMEM((chunks, n_pw, tall, wide), bf16),
            pltpu.VMEM((chunks, n_pw, tall, wide), bf16),
            pltpu.VMEM((chunks, tall, wide), f32),
            dma((2,)),
            dma((2,)),
            dma((chunks,)),
            dma((chunks,)),
            dma((chunks,)),
            dma((2, chunks)),
            dma((chunks, n_pw)),
            dma((chunks, n_pw)),
            dma((chunks, n_pw)),
            dma((chunks, n_pw)),
        ],
        compiler_params=pltpu.CompilerParams(
            collective_id=0, has_side_effects=True, vmem_limit_bytes=56 * 1024 * 1024
        ),
        cost_estimate=pl.CostEstimate(
            flops=2 * STEPS * n_res * n_band * (depth + width),
            bytes_accessed=2 * n_res * depth,
            transcendentals=0,
        ),
        name="kernel_blocks",
    )(res_pair, band_pair, coulomb[None, :], screening[None, :], val_form, cond_form, res_bands, band_bands)


def solution(mesh):
    return jax.shard_map(
        functools.partial(local, mesh.shape["blk"], mesh.shape["pw"]),
        mesh=mesh,
        in_specs=(
            P("blk", "pw"),
            P("blk", "pw"),
            P("pw"),
            P("pw"),
            P(None, "pw"),
            P(None, "pw"),
            P(None, "blk"),
            P(None, "blk"),
        ),
        out_specs=P(None, ("blk", "pw"), None),
        check_vma=False,
    )
```

```python
import functools

import jax
import jax.numpy as jnp
from jax import lax
from jax.experimental import pallas as pl
from jax.experimental.pallas import tpu as pltpu
from jax.sharding import PartitionSpec as P

NV = 200
NC = 300
STEPS = 2
LANES = 128
GROUP = 256
MESH = pl.DeviceIdType.MESH


def rounded_up(count, unit):
    return (count + unit - 1) // unit * unit


def kernel(
    n_blk, n_pw,
    res_hbm, band_ref, coul_ref, scr_ref, val_form, cond_form, res_bands, band_bands, out_ref,
    res, res_sem, val_pad, cond_pad, dens, bidx, idx_in, wgt, rhs, rhs_scr, part, up_in, dn_in, up_out, dn_out, final,
    idx_send, idx_recv, near_send, far_send, fwd_send, rhs_recv,
    up_send, up_recv, dn_send, dn_recv,
):
    chunks, rows = wgt.shape[0], wgt.shape[1]
    own_rows = out_ref.shape[1]
    me = lax.axis_index("blk")
    w = lax.axis_index("pw")
    even = lax.rem(me, 2) == 0
    one_on, two_on = lax.rem(me + 1, n_blk), lax.rem(me + 2, n_blk)
    one_back, two_back = lax.rem(me + n_blk - 1, n_blk), lax.rem(me + n_blk - 2, n_blk)

    load = pltpu.make_async_copy(res_hbm, res, res_sem)
    load.start()

    barrier = pltpu.get_barrier_semaphore()
    for other in (one_on, two_on, one_back, two_back):
        pl.semaphore_signal(barrier, inc=1, device_id=(other, w), device_id_type=MESH)

    @pl.when(w > 0)
    def _():
        pl.semaphore_signal(barrier, inc=1, device_id=(me, w - 1), device_id_type=MESH)

    @pl.when(w < n_pw - 1)
    def _():
        pl.semaphore_signal(barrier, inc=1, device_id=(me, w + 1), device_id_type=MESH)

    peers = 4 + jnp.where(w > 0, 1, 0) + jnp.where(w < n_pw - 1, 1, 0)
    pl.semaphore_wait(barrier, peers)

    def remote(src, dst, send, recv, blk, pw):
        return pltpu.make_async_remote_copy(
            src_ref=src, dst_ref=dst, send_sem=send, recv_sem=recv,
            device_id=(blk, pw), device_id_type=MESH,
        )

    def send_index(slot, target):
        return remote(bidx, idx_in.at[slot], idx_send.at[slot], idx_recv.at[slot], target, w)

    def send_near(c):
        return remote(wgt.at[c], rhs.at[0, c], near_send.at[c], rhs_recv.at[0, c], one_on, w)

    def send_far(c):
        return remote(wgt.at[c], rhs.at[1, c], far_send.at[c], rhs_recv.at[1, c], two_on, w)

    def forward(c):
        return remote(rhs.at[0, c], rhs.at[1, c], fwd_send.at[c], rhs_recv.at[1, c], one_on, w)

    def send_up(c, q):
        return remote(up_out.at[c, q], up_in.at[c, q], up_send.at[c, q], up_recv.at[c, q], me, w + 1)

    def send_dn(c, q):
        return remote(dn_out.at[c, q], dn_in.at[c, q], dn_send.at[c, q], dn_recv.at[c, q], me, w - 1)

    bidx[...] = jnp.zeros_like(bidx)
    bidx[0:1, :] = band_bands[2:3, :] * NV + band_bands[0:1, :]
    bidx[1:2, :] = band_bands[2:3, :] * NC + band_bands[1:2, :]
    send_index(0, one_on).start()
    send_index(1, two_on).start()

    @pl.loop(0, chunks)
    def _(c):
        block = band_ref[pl.ds(pl.multiple_of(c * rows, rows), rows), :].astype(jnp.float32)
        wgt[c] = (block * (2.0 * coul_ref[...])).astype(jnp.bfloat16)
        send_near(c).start()

        @pl.when(even)
        def _():
            send_far(c).start()

    for form, padded in ((val_form, val_pad), (cond_form, cond_pad)):
        spare = jnp.zeros((padded.shape[0] - form.shape[0], form.shape[1]), jnp.float32)
        padded[...] = jnp.concatenate([form[...].astype(jnp.float32), spare], axis=0).astype(padded.dtype)

    def one_hot(row, depth):
        column = jnp.concatenate(
            [
                jnp.broadcast_to(row[:, h * LANES:(h + 1) * LANES], (LANES, LANES)).T
                for h in range(GROUP // LANES)
            ],
            axis=0,
        )
        lane = lax.broadcasted_iota(jnp.int32, (GROUP, LANES), 1)
        return jnp.concatenate(
            [
                jnp.where(column == lane + start, 1.0, 0.0).astype(jnp.bfloat16)
                for start in range(0, depth, LANES)
            ],
            axis=1,
        )

    def density(val_row, cond_row):
        valence = jnp.dot(
            one_hot(val_row, val_pad.shape[0]), val_pad[...], preferred_element_type=jnp.float32
        )
        conduct = jnp.dot(
            one_hot(cond_row, cond_pad.shape[0]), cond_pad[...], preferred_element_type=jnp.float32
        )
        return (valence * conduct).astype(jnp.bfloat16)

    def fill(g):
        at = pl.ds(pl.multiple_of(g * GROUP, GROUP), GROUP)
        point = res_bands[2:3, at]
        dens[at, :] = density(point * NV + res_bands[0:1, at], point * NC + res_bands[1:2, at])

    by_block = own_rows % GROUP == 0

    @pl.when(even if by_block else me >= 0)
    def _():
        @pl.loop(0, dens.shape[0] // GROUP)
        def _(g):
            fill(g)

    for slot, target in ((0, one_on), (1, two_on)):
        send_index(slot, target).wait_recv()
        for g in range(chunks * rows // GROUP):
            at = slice(g * GROUP, (g + 1) * GROUP)
            block = density(idx_in[slot, 0:1, at], idx_in[slot, 1:2, at])
            block = (block.astype(jnp.float32) * (-scr_ref[...])).astype(jnp.bfloat16)
            for h in range(GROUP // rows):
                rhs_scr[slot, g * (GROUP // rows) + h] = block[h * rows:(h + 1) * rows, :]

    load.wait()

    half = chunks // 2

    def parts_of(c):
        slot, unit = c // half, 2 * (c % half)
        return (
            (jnp.where(even, 0, slot), jnp.where(even, c, unit)),
            (jnp.where(even, 1, slot), jnp.where(even, c, unit + 1)),
        )

    def landed(slot, unit):
        remote(wgt.at[0], rhs.at[slot, unit], near_send.at[0], rhs_recv.at[slot, unit], one_on, w).wait_recv()

    def packed(term):
        if 2 * rows >= LANES:
            return term
        fold = LANES // (2 * rows)
        tall = own_rows // fold
        return jnp.concatenate([term[f * tall:(f + 1) * tall] for f in range(fold)], axis=1)

    def multiply(group):
        places = []
        for c in group:
            first, second = parts_of(c)
            landed(*first)

            @pl.when(even)
            def _():
                forward(c).start()

            landed(*second)
            places += [first, second]
        weighted = jnp.concatenate([rhs[place] for place in places], axis=0)
        screened = jnp.concatenate([rhs_scr[place] for place in places], axis=0)

        @pl.loop(0, n_pw)
        def _(j):
            q = jnp.where(2 * w < n_pw, n_pw - 1 - j, j)
            at = pl.ds(pl.multiple_of(q * own_rows, own_rows), own_rows)
            if by_block and group[0] == 0:
                @pl.when(jnp.logical_not(even))
                def _():
                    @pl.loop(0, own_rows // GROUP)
                    def _(g):
                        fill(q * (own_rows // GROUP) + g)

            contract = (((1,), (1,)), ((), ()))
            term = lax.dot_general(
                res[at, :], weighted, contract, preferred_element_type=jnp.float32
            ) + lax.dot_general(
                dens[at, :], screened, contract, preferred_element_type=jnp.float32
            )
            terms = [
                packed(term[:, k * 2 * rows:(k + 1) * 2 * rows]) for k in range(len(group))
            ]
            for c, piece in zip(group, terms):
                part[c, q] = piece

            @pl.when(jnp.logical_and(w == 0, q > 0))
            def _():
                for c, piece in zip(group, terms):
                    up_out[c, q] = piece.astype(jnp.bfloat16)
                    send_up(c, q).start()

            @pl.when(jnp.logical_and(w == n_pw - 1, q < n_pw - 1))
            def _():
                for c, piece in zip(group, terms):
                    dn_out[c, q] = piece.astype(jnp.bfloat16)
                    send_dn(c, q).start()

    def upward(c):
        @pl.when(w > 0)
        def _():
            @pl.loop(0, n_pw - 1 - w)
            def _(j):
                q = n_pw - 1 - j
                send_up(c, q).wait_recv()
                total = part[c, q] + up_in[c, q].astype(jnp.float32)
                up_out[c, q] = total.astype(jnp.bfloat16)
                send_up(c, q).start()

    def downward(c):
        @pl.when(w < n_pw - 1)
        def _():
            @pl.loop(0, w)
            def _(q):
                send_dn(c, q).wait_recv()
                total = part[c, q] + dn_in[c, q].astype(jnp.float32)
                dn_out[c, q] = total.astype(jnp.bfloat16)
                send_dn(c, q).start()

    def relay_near_end(c):
        @pl.when(2 * w < n_pw)
        def _():
            upward(c)

        @pl.when(2 * w >= n_pw)
        def _():
            downward(c)

    def relay_rest(c):
        @pl.when(2 * w < n_pw)
        def _():
            downward(c)

        @pl.when(2 * w >= n_pw)
        def _():
            upward(c)

        final[c] = part[c, w]

        @pl.when(w > 0)
        def _():
            send_up(c, w).wait_recv()
            final[c] += up_in[c, w].astype(jnp.float32)

        @pl.when(w < n_pw - 1)
        def _():
            send_dn(c, w).wait_recv()
            final[c] += dn_in[c, w].astype(jnp.float32)

    groups = [(0, 1)] + [(c,) for c in range(2, chunks)]
    late = []
    for group in groups:
        multiply(group)
        for c in group:
            relay_near_end(c)
        for c in late:
            relay_rest(c)
        late = group
    for c in late:
        relay_rest(c)

    tall = final.shape[1]

    def write(c, place):
        for f in range(own_rows // tall):
            block = final[c][:, f * 2 * rows:(f + 1) * 2 * rows]
            for h in range(2):
                s, unit = place[h]
                out_ref[s, f * tall:(f + 1) * tall, unit * rows:(unit + 1) * rows] = (
                    block[:, h * rows:(h + 1) * rows]
                )

    @pl.when(even)
    def _():
        for c in range(chunks):
            write(c, ((0, c), (1, c)))

    @pl.when(jnp.logical_not(even))
    def _():
        for c in range(chunks):
            slot, unit = c // half, 2 * (c % half)
            write(c, ((slot, unit), (slot, unit + 1)))

    send_index(0, one_on).wait_send()
    send_index(1, two_on).wait_send()

    @pl.loop(0, chunks)
    def _(c):
        send_near(c).wait_send()

        @pl.when(even)
        def _():
            send_far(c).wait_send()
            forward(c).wait_send()

        @pl.when(w < n_pw - 1)
        def _():
            @pl.loop(w + 1, n_pw)
            def _(q):
                send_up(c, q).wait_send()

        @pl.when(w > 0)
        def _():
            @pl.loop(0, w)
            def _(q):
                send_dn(c, q).wait_send()


def local(n_blk, n_pw, res_pair, band_pair, coulomb, screening, val_form, cond_form, res_bands, band_bands):
    n_res, depth = res_pair.shape
    n_band = band_pair.shape[0]
    width = val_form.shape[1]
    n_val, n_cond = val_form.shape[0], cond_form.shape[0]
    chunks = 4 if n_pw <= 4 else 2
    rows = n_band // chunks
    own_rows = n_res // n_pw
    fold = max(1, LANES // (2 * rows))
    tall, wide = own_rows // fold, 2 * rows * fold
    bf16, f32, i32 = jnp.bfloat16, jnp.float32, jnp.int32
    dma = pltpu.SemaphoreType.DMA
    vmem = pl.BlockSpec(memory_space=pltpu.VMEM)
    return pl.pallas_call(
        functools.partial(kernel, n_blk, n_pw),
        out_shape=jax.ShapeDtypeStruct((STEPS, own_rows, n_band), f32),
        in_specs=[pl.BlockSpec(memory_space=pl.ANY)] + [vmem] * 7,
        out_specs=vmem,
        scratch_shapes=[
            pltpu.VMEM((n_res, depth), bf16),
            dma(()),
            pltpu.VMEM((rounded_up(n_val, LANES), width), bf16),
            pltpu.VMEM((rounded_up(n_cond, LANES), width), bf16),
            pltpu.VMEM((n_res, width), bf16),
            pltpu.VMEM((8, n_band), i32),
            pltpu.VMEM((2, 8, n_band), i32),
            pltpu.VMEM((chunks, rows, depth), bf16),
            pltpu.VMEM((2, chunks, rows, depth), bf16),
            pltpu.VMEM((2, chunks, rows, width), bf16),
            pltpu.VMEM((chunks, n_pw, tall, wide), f32),
            pltpu.VMEM((chunks, n_pw, tall, wide), bf16),
            pltpu.VMEM((chunks, n_pw, tall, wide), bf16),
            pltpu.VMEM((chunks, n_pw, tall, wide), bf16),
            pltpu.VMEM((chunks, n_pw, tall, wide), bf16),
            pltpu.VMEM((chunks, tall, wide), f32),
            dma((2,)),
            dma((2,)),
            dma((chunks,)),
            dma((chunks,)),
            dma((chunks,)),
            dma((2, chunks)),
            dma((chunks, n_pw)),
            dma((chunks, n_pw)),
            dma((chunks, n_pw)),
            dma((chunks, n_pw)),
        ],
        compiler_params=pltpu.CompilerParams(
            collective_id=0, has_side_effects=True, vmem_limit_bytes=56 * 1024 * 1024
        ),
        cost_estimate=pl.CostEstimate(
            flops=2 * STEPS * n_res * n_band * (depth + width),
            bytes_accessed=2 * n_res * depth,
            transcendentals=0,
        ),
        name="kernel_blocks",
    )(res_pair, band_pair, coulomb[None, :], screening[None, :], val_form, cond_form, res_bands, band_bands)


def solution(mesh):
    return jax.shard_map(
        functools.partial(local, mesh.shape["blk"], mesh.shape["pw"]),
        mesh=mesh,
        in_specs=(
            P("blk", "pw"),
            P("blk", "pw"),
            P("pw"),
            P("pw"),
            P(None, "pw"),
            P(None, "pw"),
            P(None, "blk"),
            P(None, "blk"),
        ),
        out_specs=P(None, ("blk", "pw"), None),
        check_vma=False,
    )
```

```python
import functools

import jax
import jax.numpy as jnp
from jax import lax
from jax.experimental import pallas as pl
from jax.experimental.pallas import tpu as pltpu
from jax.sharding import PartitionSpec as P

NV = 200
NC = 300
STEPS = 2
LANES = 128
GROUP = 256
MESH = pl.DeviceIdType.MESH


def rounded_up(count, unit):
    return (count + unit - 1) // unit * unit


def kernel(
    n_blk, n_pw,
    res_hbm, band_ref, coul_ref, scr_ref, val_form, cond_form, res_bands, band_bands, out_ref,
    res, res_sem, val_pad, cond_pad, dens, bidx, idx_in, wgt, rhs, rhs_scr, part, up_in, dn_in, up_out, dn_out, final,
    idx_send, idx_recv, near_send, far_send, fwd_send, rhs_recv,
    up_send, up_recv, dn_send, dn_recv,
):
    chunks, rows = wgt.shape[0], wgt.shape[1]
    own_rows = out_ref.shape[1]
    me = lax.axis_index("blk")
    w = lax.axis_index("pw")
    even = lax.rem(me, 2) == 0
    one_on, two_on = lax.rem(me + 1, n_blk), lax.rem(me + 2, n_blk)
    one_back, two_back = lax.rem(me + n_blk - 1, n_blk), lax.rem(me + n_blk - 2, n_blk)

    load = pltpu.make_async_copy(res_hbm, res, res_sem)
    load.start()

    barrier = pltpu.get_barrier_semaphore()
    for other in (one_on, two_on, one_back, two_back):
        pl.semaphore_signal(barrier, inc=1, device_id=(other, w), device_id_type=MESH)

    @pl.when(w > 0)
    def _():
        pl.semaphore_signal(barrier, inc=1, device_id=(me, w - 1), device_id_type=MESH)

    @pl.when(w < n_pw - 1)
    def _():
        pl.semaphore_signal(barrier, inc=1, device_id=(me, w + 1), device_id_type=MESH)

    peers = 4 + jnp.where(w > 0, 1, 0) + jnp.where(w < n_pw - 1, 1, 0)
    pl.semaphore_wait(barrier, peers)

    def remote(src, dst, send, recv, blk, pw):
        return pltpu.make_async_remote_copy(
            src_ref=src, dst_ref=dst, send_sem=send, recv_sem=recv,
            device_id=(blk, pw), device_id_type=MESH,
        )

    def send_index(slot, target):
        return remote(bidx, idx_in.at[slot], idx_send.at[slot], idx_recv.at[slot], target, w)

    def send_near(c):
        return remote(wgt.at[c], rhs.at[0, c], near_send.at[c], rhs_recv.at[0, c], one_on, w)

    def send_far(c):
        return remote(wgt.at[c], rhs.at[1, c], far_send.at[c], rhs_recv.at[1, c], two_on, w)

    def forward(c):
        return remote(rhs.at[0, c], rhs.at[1, c], fwd_send.at[c], rhs_recv.at[1, c], one_on, w)

    def send_up(c, q):
        return remote(up_out.at[c, q], up_in.at[c, q], up_send.at[c, q], up_recv.at[c, q], me, w + 1)

    def send_dn(c, q):
        return remote(dn_out.at[c, q], dn_in.at[c, q], dn_send.at[c, q], dn_recv.at[c, q], me, w - 1)

    bidx[...] = jnp.zeros_like(bidx)
    bidx[0:1, :] = band_bands[2:3, :] * NV + band_bands[0:1, :]
    bidx[1:2, :] = band_bands[2:3, :] * NC + band_bands[1:2, :]
    send_index(0, one_on).start()
    send_index(1, two_on).start()

    @pl.loop(0, chunks)
    def _(c):
        block = band_ref[pl.ds(pl.multiple_of(c * rows, rows), rows), :].astype(jnp.float32)
        wgt[c] = (block * (2.0 * coul_ref[...])).astype(jnp.bfloat16)
        send_near(c).start()

        @pl.when(even)
        def _():
            send_far(c).start()

    for form, padded in ((val_form, val_pad), (cond_form, cond_pad)):
        spare = jnp.zeros((padded.shape[0] - form.shape[0], form.shape[1]), jnp.float32)
        padded[...] = jnp.concatenate([form[...].astype(jnp.float32), spare], axis=0).astype(padded.dtype)

    def one_hot(row, depth):
        column = jnp.concatenate(
            [
                jnp.broadcast_to(row[:, h * LANES:(h + 1) * LANES], (LANES, LANES)).T
                for h in range(GROUP // LANES)
            ],
            axis=0,
        )
        lane = lax.broadcasted_iota(jnp.int32, (GROUP, LANES), 1)
        return jnp.concatenate(
            [
                jnp.where(column == lane + start, 1.0, 0.0).astype(jnp.bfloat16)
                for start in range(0, depth, LANES)
            ],
            axis=1,
        )

    def density(val_row, cond_row):
        valence = jnp.dot(
            one_hot(val_row, val_pad.shape[0]), val_pad[...], preferred_element_type=jnp.float32
        )
        conduct = jnp.dot(
            one_hot(cond_row, cond_pad.shape[0]), cond_pad[...], preferred_element_type=jnp.float32
        )
        return (valence * conduct).astype(jnp.bfloat16)

    @pl.loop(0, dens.shape[0] // GROUP)
    def _(g):
        at = pl.ds(pl.multiple_of(g * GROUP, GROUP), GROUP)
        point = res_bands[2:3, at]
        dens[at, :] = density(point * NV + res_bands[0:1, at], point * NC + res_bands[1:2, at])

    for slot, target in ((0, one_on), (1, two_on)):
        send_index(slot, target).wait_recv()
        for g in range(chunks * rows // GROUP):
            at = slice(g * GROUP, (g + 1) * GROUP)
            block = density(idx_in[slot, 0:1, at], idx_in[slot, 1:2, at])
            block = (block.astype(jnp.float32) * (-scr_ref[...])).astype(jnp.bfloat16)
            for h in range(GROUP // rows):
                rhs_scr[slot, g * (GROUP // rows) + h] = block[h * rows:(h + 1) * rows, :]

    load.wait()

    half = chunks // 2

    def parts_of(c):
        slot, unit = c // half, 2 * (c % half)
        return (
            (jnp.where(even, 0, slot), jnp.where(even, c, unit)),
            (jnp.where(even, 1, slot), jnp.where(even, c, unit + 1)),
        )

    def landed(slot, unit):
        remote(wgt.at[0], rhs.at[slot, unit], near_send.at[0], rhs_recv.at[slot, unit], one_on, w).wait_recv()

    def packed(term):
        if 2 * rows >= LANES:
            return term
        fold = LANES // (2 * rows)
        tall = own_rows // fold
        return jnp.concatenate([term[f * tall:(f + 1) * tall] for f in range(fold)], axis=1)

    def multiply(group):
        places = []
        for c in group:
            first, second = parts_of(c)
            landed(*first)

            @pl.when(even)
            def _():
                forward(c).start()

            landed(*second)
            places += [first, second]
        weighted = jnp.concatenate([rhs[place] for place in places], axis=0)
        screened = jnp.concatenate([rhs_scr[place] for place in places], axis=0)

        @pl.loop(0, n_pw)
        def _(j):
            q = jnp.where(2 * w < n_pw, n_pw - 1 - j, j)
            at = pl.ds(pl.multiple_of(q * own_rows, own_rows), own_rows)
            contract = (((1,), (1,)), ((), ()))
            term = lax.dot_general(
                res[at, :], weighted, contract, preferred_element_type=jnp.float32
            ) + lax.dot_general(
                dens[at, :], screened, contract, preferred_element_type=jnp.float32
            )
            terms = [
                packed(term[:, k * 2 * rows:(k + 1) * 2 * rows]) for k in range(len(group))
            ]
            for c, piece in zip(group, terms):
                part[c, q] = piece

            @pl.when(jnp.logical_and(w == 0, q > 0))
            def _():
                for c, piece in zip(group, terms):
                    up_out[c, q] = piece.astype(jnp.bfloat16)
                    send_up(c, q).start()

            @pl.when(jnp.logical_and(w == n_pw - 1, q < n_pw - 1))
            def _():
                for c, piece in zip(group, terms):
                    dn_out[c, q] = piece.astype(jnp.bfloat16)
                    send_dn(c, q).start()

    def upward(c):
        @pl.when(w > 0)
        def _():
            @pl.loop(0, n_pw - 1 - w)
            def _(j):
                q = n_pw - 1 - j
                send_up(c, q).wait_recv()
                total = part[c, q] + up_in[c, q].astype(jnp.float32)
                up_out[c, q] = total.astype(jnp.bfloat16)
                send_up(c, q).start()

    def downward(c):
        @pl.when(w < n_pw - 1)
        def _():
            @pl.loop(0, w)
            def _(q):
                send_dn(c, q).wait_recv()
                total = part[c, q] + dn_in[c, q].astype(jnp.float32)
                dn_out[c, q] = total.astype(jnp.bfloat16)
                send_dn(c, q).start()

    def relay_near_end(c):
        @pl.when(2 * w < n_pw)
        def _():
            upward(c)

        @pl.when(2 * w >= n_pw)
        def _():
            downward(c)

    def relay_rest(c):
        @pl.when(2 * w < n_pw)
        def _():
            downward(c)

        @pl.when(2 * w >= n_pw)
        def _():
            upward(c)

        final[c] = part[c, w]

        @pl.when(w > 0)
        def _():
            send_up(c, w).wait_recv()
            final[c] += up_in[c, w].astype(jnp.float32)

        @pl.when(w < n_pw - 1)
        def _():
            send_dn(c, w).wait_recv()
            final[c] += dn_in[c, w].astype(jnp.float32)

    groups = [(0, 1, 2, 3), (4, 5, 6), (7,)] if chunks == 8 else [tuple(range(chunks))]
    late = []
    for group in groups:
        multiply(group)
        for c in group:
            relay_near_end(c)
        for c in late:
            relay_rest(c)
        late = group
    for c in late:
        relay_rest(c)

    tall = final.shape[1]

    def write(c, place):
        for f in range(own_rows // tall):
            block = final[c][:, f * 2 * rows:(f + 1) * 2 * rows]
            for h in range(2):
                s, unit = place[h]
                out_ref[s, f * tall:(f + 1) * tall, unit * rows:(unit + 1) * rows] = (
                    block[:, h * rows:(h + 1) * rows]
                )

    @pl.when(even)
    def _():
        for c in range(chunks):
            write(c, ((0, c), (1, c)))

    @pl.when(jnp.logical_not(even))
    def _():
        for c in range(chunks):
            slot, unit = c // half, 2 * (c % half)
            write(c, ((slot, unit), (slot, unit + 1)))

    send_index(0, one_on).wait_send()
    send_index(1, two_on).wait_send()

    @pl.loop(0, chunks)
    def _(c):
        send_near(c).wait_send()

        @pl.when(even)
        def _():
            send_far(c).wait_send()
            forward(c).wait_send()

        @pl.when(w < n_pw - 1)
        def _():
            @pl.loop(w + 1, n_pw)
            def _(q):
                send_up(c, q).wait_send()

        @pl.when(w > 0)
        def _():
            @pl.loop(0, w)
            def _(q):
                send_dn(c, q).wait_send()


def local(n_blk, n_pw, res_pair, band_pair, coulomb, screening, val_form, cond_form, res_bands, band_bands):
    n_res, depth = res_pair.shape
    n_band = band_pair.shape[0]
    width = val_form.shape[1]
    n_val, n_cond = val_form.shape[0], cond_form.shape[0]
    chunks = 8 if n_pw <= 4 else 2
    rows = n_band // chunks
    own_rows = n_res // n_pw
    fold = max(1, LANES // (2 * rows))
    tall, wide = own_rows // fold, 2 * rows * fold
    bf16, f32, i32 = jnp.bfloat16, jnp.float32, jnp.int32
    dma = pltpu.SemaphoreType.DMA
    vmem = pl.BlockSpec(memory_space=pltpu.VMEM)
    return pl.pallas_call(
        functools.partial(kernel, n_blk, n_pw),
        out_shape=jax.ShapeDtypeStruct((STEPS, own_rows, n_band), f32),
        in_specs=[pl.BlockSpec(memory_space=pl.ANY)] + [vmem] * 7,
        out_specs=vmem,
        scratch_shapes=[
            pltpu.VMEM((n_res, depth), bf16),
            dma(()),
            pltpu.VMEM((rounded_up(n_val, LANES), width), bf16),
            pltpu.VMEM((rounded_up(n_cond, LANES), width), bf16),
            pltpu.VMEM((n_res, width), bf16),
            pltpu.VMEM((8, n_band), i32),
            pltpu.VMEM((2, 8, n_band), i32),
            pltpu.VMEM((chunks, rows, depth), bf16),
            pltpu.VMEM((2, chunks, rows, depth), bf16),
            pltpu.VMEM((2, chunks, rows, width), bf16),
            pltpu.VMEM((chunks, n_pw, tall, wide), f32),
            pltpu.VMEM((chunks, n_pw, tall, wide), bf16),
            pltpu.VMEM((chunks, n_pw, tall, wide), bf16),
            pltpu.VMEM((chunks, n_pw, tall, wide), bf16),
            pltpu.VMEM((chunks, n_pw, tall, wide), bf16),
            pltpu.VMEM((chunks, tall, wide), f32),
            dma((2,)),
            dma((2,)),
            dma((chunks,)),
            dma((chunks,)),
            dma((chunks,)),
            dma((2, chunks)),
            dma((chunks, n_pw)),
            dma((chunks, n_pw)),
            dma((chunks, n_pw)),
            dma((chunks, n_pw)),
        ],
        compiler_params=pltpu.CompilerParams(
            collective_id=0, has_side_effects=True, vmem_limit_bytes=56 * 1024 * 1024
        ),
        cost_estimate=pl.CostEstimate(
            flops=2 * STEPS * n_res * n_band * (depth + width),
            bytes_accessed=2 * n_res * depth,
            transcendentals=0,
        ),
        name="kernel_blocks",
    )(res_pair, band_pair, coulomb[None, :], screening[None, :], val_form, cond_form, res_bands, band_bands)


def solution(mesh):
    return jax.shard_map(
        functools.partial(local, mesh.shape["blk"], mesh.shape["pw"]),
        mesh=mesh,
        in_specs=(
            P("blk", "pw"),
            P("blk", "pw"),
            P("pw"),
            P("pw"),
            P(None, "pw"),
            P(None, "pw"),
            P(None, "blk"),
            P(None, "blk"),
        ),
        out_specs=P(None, ("blk", "pw"), None),
        check_vma=False,
    )
```
